256 devices in a mesh: dp: 32 (over z, y), expert: 8 (over x, core).
Axes of the slice: x: 4, y: 4, z: 8, core: 2. Of those that a mesh axis runs over, the one named last changes fastest.
Arguments:
- tokens: bfloat16 [1024, 4096], P(('dp', 'expert')), may hold values from -6 to 6
- out_grad: bfloat16 [1024, 4096], P(('dp', 'expert')), may hold values from -6 to 6
- token_flags: int32 [1024], P(('dp', 'expert')), may hold values 0 or 1
- routes: int32 [1024, 2], P(('dp', 'expert')), may hold values from 0 to 7, all different within a row; in each aligned block of 4 rows (0 to 3, 4 to 7, ...) at most 2 rows name the same one
- route_logits: float32 [1024, 2], P(('dp', 'expert')), may hold values from -6 to 6
- gate_weight: bfloat16 [8, 4096, 8192], P('expert', None, 'dp'), may hold values from -0.09375 to 0.09375
- up_weight: bfloat16 [8, 4096, 8192], P('expert', None, 'dp'), may hold values from -0.09375 to 0.09375
- down_weight: bfloat16 [8, 8192, 4096], P('expert', 'dp'), may hold values from -0.0625 to 0.0625
- query_states: bfloat16 [8, 128, 32, 4096], P('expert', 'dp'), may hold values from -5 to 5, as said below
- query_len: int32 [8, 128], P('expert', 'dp'), may hold values from 1 to 32
- doc_states: bfloat16 [8, 128, 32, 4096], P('expert', 'dp'), may hold values from -5 to 5, as said below
- doc_len: int32 [8, 128], P('expert', 'dp'), may hold values from 1 to 32
- query_pos: int32 [8, 128], P('expert', 'dp'), may hold values from 0 to 127, each once within a row
Outputs:
- token_grads: bfloat16 [1024, 4096], P(('dp', 'expert'))
- logit_grads: float32 [1024, 2], P(('dp', 'expert'))
- query_grads: bfloat16 [8, 128, 32, 4096], P('expert', 'dp')
- doc_grads: bfloat16 [8, 128, 32, 4096], P('expert', 'dp')
- loss: float32 [], replicated
The draws below stay inside these ranges and needn't reach their ends.
Inputs may be any that keep to these rules, and one draw needn't show every extreme that they name: `routes`: among the rows of one device, no expert is named by more than 2 of them; some expert reaches 2. The two experts of a token differ. `query_pos`: each group's row names every document of the group once. `query_states`: hidden states of order one. `doc_states`: hidden states of order one.
All inputs are finite; a program needn't handle non-finite values. No bound on the sum of `token_flags` on one device may be relied on, other than what follows from the above.
Results may differ from the reference program's by a relative error of at most 0.012.
Values may be sent and summed in bfloat16 or wider, within the bound.
No kernel may reach another device: no remote copies, remote signals or barrier semaphores. Data moves between devices by JAX's collectives and lax.ppermute only.
A program may use at most 64 MiB of HBM per device.

```python
import math
import jax
import jax.numpy as jnp
import numpy as np
from jax import lax

D = 4096
FF = 8192
EXPERTS = 8
T_DEV = 4
TOKENS = 1024
CAP = 2
GROUPS = 8
GQ = 128
PLEN = 32
N_DP = 32
N_EXPERT = 8


def draw_query_states(key, part):
    key = jax.random.fold_in(key, 7)
    base = jnp.clip(jax.random.normal(key, (GROUPS, GQ, PLEN, D), jnp.float32), -5.0, 5.0)
    return base.astype(jnp.bfloat16)


def draw_doc_states(key, part):
    key = jax.random.fold_in(key, 13)
    base = jnp.clip(jax.random.normal(key, (GROUPS, GQ, PLEN, D), jnp.float32), -5.0, 5.0)
    return base.astype(jnp.bfloat16)


def touch_ends(values, key, smallest, largest):
    place = [jax.random.randint(jax.random.fold_in(key, axis), (), 0, length) for axis, length in enumerate(values.shape)]
    widest = values.shape.index(max(values.shape))
    next_to = place[:widest] + [(place[widest] + 1) % values.shape[widest]] + place[widest + 1:]
    return values.at[tuple(place)].set(smallest).at[tuple(next_to)].set(largest)


def block_levels(rng, extent, cuts, low, high):
    factor_of, own = 1.0, jax.random.fold_in(rng, 6)
    for axis_at, shards_of in cuts:
        steps = jnp.exp(jax.random.uniform(jax.random.fold_in(own, axis_at), (shards_of,), jnp.float32, low / len(cuts), high / len(cuts)))
        factor_of = factor_of * jnp.repeat(steps, extent[axis_at] // shards_of).reshape([-1 if axis == axis_at else 1 for axis in range(len(extent))])
    return factor_of


def assign_block(stream_key, own, number, rows, number_of, top, limit, slope):
    sequence = jax.random.permutation(stream_key, number_of)
    packed, usual = shares(number_of, rows * top, limit, slope, True), shares(number_of, rows * top, limit, slope, False)
    places = jnp.arange(number_of)

    def named(sizes, rotation):
        used = int((sizes > 0).sum())
        fixed = max(1, used // 4)
        shifted = fixed + (places - fixed + rotation * (used - fixed)) % max(1, number_of - fixed)
        return jnp.zeros((number_of,), jnp.int32).at[sequence[jnp.where(places < fixed, places, shifted)]].set(jnp.asarray(sizes, jnp.int32))

    sizes = jnp.where(number % 4 == 0, named(packed, number // 4), named(usual, number - number // 4 - 1))
    mixed = jax.random.permutation(jax.random.fold_in(own, 3), number_of)
    donor, taker = mixed[0:number_of // 2 * 2:2], mixed[1:number_of // 2 * 2:2]
    margin = jnp.minimum(sizes[donor] - 1, limit - sizes[taker]) // 2
    margin = jnp.where((donor == sequence[0]) | (taker == sequence[0]) | (sizes[taker] == 0), 0, jnp.maximum(margin, 0))
    shifted = jax.random.randint(jax.random.fold_in(own, 4), (number_of // 2,), 0, 1 << 20) % (margin + 1)
    sizes = sizes.at[donor].add(-shifted).at[taker].add(shifted)
    labels = jnp.searchsorted(jnp.cumsum(sizes), jnp.arange(rows * top), side="right").astype(jnp.int32)
    grid = labels.reshape(top, rows).T
    grid = grid[jax.random.permutation(jax.random.fold_in(own, 1), rows)]
    rotation = jax.random.randint(jax.random.fold_in(own, 2), (rows, 1), 0, top)
    return jnp.take_along_axis(grid, (jnp.arange(top)[None, :] + rotation) % top, axis=1)


def shares(number_of, total, reach, skew, full):
    portions = [(1 << 20) // math.isqrt(standing ** skew) + 1 for standing in range(1, number_of + 1)]
    largest = reach if full else min(reach, max(-(-total // number_of), total * portions[0] // sum(portions)))
    least = 1 if total - largest >= number_of - 1 else 0
    given, spare = [largest] + [least] * (number_of - 1), total - largest - least * (number_of - 1)
    while spare > 0:
        free = [i for i in range(1, number_of) if given[i] < largest] or [i for i in range(1, number_of) if given[i] < reach]
        mass, budget = sum([portions[i] for i in free]), spare
        for i in free:
            addition = min(reach - given[i], max(1, budget * portions[i] // mass), spare)
            given[i] = given[i] + addition
            spare = spare - addition
    return np.array(given)


def normal_values(key, extent, deviation, limit, shards=(), kind=jnp.bfloat16):
    values = deviation * jax.random.normal(key, extent, jnp.float32)
    if shards:
        values = values * block_levels(key, extent, shards, -0.22, 0.18)
    return jnp.clip(values, -limit, limit).astype(kind)


def setup_inputs(seed: int = 0) -> dict:
    keys = jax.random.split(jax.random.key(seed), 14)
    tokens = normal_values(keys[0], (TOKENS, D), 1.0, 6.0, ((0, 256),))
    out_grad = normal_values(keys[1], (TOKENS, D), 1.0, 6.0, ((0, 256),))
    token_flags = touch_ends((jax.random.randint(keys[2], (TOKENS,), 0, 4) < 1).astype(jnp.int32), jax.random.fold_in(keys[2], 1), 0, 1)
    routes_keys = jax.random.split(jax.random.fold_in(keys[3], 1), TOKENS // T_DEV)
    routes_turns = jax.random.permutation(jax.random.fold_in(keys[3], 3), TOKENS // T_DEV)
    routes = jax.vmap(lambda own, number: assign_block(jax.random.fold_in(keys[3], 2), own, number, T_DEV, EXPERTS, 2, CAP, 2))(routes_keys, routes_turns).reshape((TOKENS, 2))
    route_logits = normal_values(keys[4], (TOKENS, 2), 1.5, 6.0, ((0, 256),), jnp.float32)
    gate_weight = normal_values(keys[5], (EXPERTS, D, FF), D ** -0.5, 0.09375, ((0, 8), (2, 32)))
    up_weight = normal_values(keys[6], (EXPERTS, D, FF), D ** -0.5, 0.09375, ((0, 8), (2, 32)))
    down_weight = normal_values(keys[7], (EXPERTS, FF, D), FF ** -0.5, 0.0625, ((0, 8), (1, 32)))
    query_states = draw_query_states(jax.random.fold_in(keys[13], 71), 0)
    query_len = touch_ends(jax.random.randint(keys[9], (GROUPS, GQ), 1, PLEN + 1), jax.random.fold_in(keys[9], 1), 1, PLEN).astype(jnp.int32)
    doc_states = draw_doc_states(jax.random.fold_in(keys[13], 71), 0)
    doc_len = touch_ends(jax.random.randint(keys[11], (GROUPS, GQ), 1, PLEN + 1), jax.random.fold_in(keys[11], 1), 1, PLEN).astype(jnp.int32)
    query_pos = jax.vmap(lambda own: jax.random.permutation(own, GQ))(jax.random.split(keys[12], GROUPS)).reshape((GROUPS, GQ)).astype(jnp.int32)
    return {"tokens": tokens, "out_grad": out_grad, "token_flags": token_flags, "routes": routes, "route_logits": route_logits, "gate_weight": gate_weight, "up_weight": up_weight, "down_weight": down_weight, "query_states": query_states, "query_len": query_len, "doc_states": doc_states, "doc_len": doc_len, "query_pos": query_pos}


def pooled(states, lengths):
    valid = (jnp.arange(PLEN, dtype=jnp.int32)[None, :] < lengths[:, None]).astype(jnp.float32)
    summed = jnp.einsum('qt,qtd->qd', valid, states.astype(jnp.float32))
    return ((summed / lengths[:, None].astype(jnp.float32)).astype(jnp.bfloat16), valid)

def one_group(inputs):
    q_states, q_length, d_states, d_length, q_target = inputs
    scale_factor = 1.0 / (0.02 * math.sqrt(D))
    query_emb, q_valid = pooled(q_states, q_length)
    doc_emb, d_valid = pooled(d_states, d_length)
    scores = jnp.dot(query_emb, doc_emb.T, preferred_element_type=jnp.float32) * scale_factor
    top = lax.optimization_barrier(jnp.max(scores, axis=1, keepdims=True))
    expo = jnp.exp(scores - top)
    total = lax.optimization_barrier(jnp.sum(expo, axis=1, keepdims=True))
    probs = expo / total
    lse = top[:, 0] + jnp.log(total[:, 0])
    targets = jnp.arange(GQ, dtype=jnp.int32)[None, :] == q_target[:, None]
    positive = lax.optimization_barrier(jnp.sum(jnp.where(targets, scores, 0.0), axis=1))
    loss_sum = jnp.sum(lse - positive)
    coef = (probs - targets.astype(jnp.float32)).astype(jnp.bfloat16)
    query_emb_grad = jnp.dot(coef, doc_emb, preferred_element_type=jnp.float32) * scale_factor
    doc_emb_grad = jnp.dot(coef.T, query_emb, preferred_element_type=jnp.float32) * scale_factor
    q_out = ((query_emb_grad / q_length[:, None].astype(jnp.float32))[:, None, :] * q_valid[:, :, None]).astype(jnp.bfloat16)
    d_out = ((doc_emb_grad / d_length[:, None].astype(jnp.float32))[:, None, :] * d_valid[:, :, None]).astype(jnp.bfloat16)
    return (loss_sum, q_out, d_out)

def reference(tokens, out_grad, token_flags, routes, route_logits, gate_weight, up_weight, down_weight, query_states, query_len, doc_states, doc_len, query_pos):
    blocks = N_DP * N_EXPERT
    rows_all = blocks * CAP
    mix = jax.nn.softmax(route_logits, axis=-1)
    cotangent = jnp.where(token_flags[:, None] == 0, out_grad, jnp.zeros_like(out_grad))
    block_routes = routes.reshape(blocks, T_DEV * 2)
    member = (block_routes[:, :, None] == jnp.arange(EXPERTS, dtype=jnp.int32)[None, None, :]).astype(jnp.int32)
    earlier = jnp.cumsum(member, axis=1) - member
    ranks = lax.optimization_barrier(jnp.sum(earlier * member, axis=2))
    slots = (jnp.arange(blocks, dtype=jnp.int32)[:, None] * CAP + ranks).reshape(-1).astype(jnp.int32)
    assigned = routes.reshape(-1)
    spread_tok = jnp.repeat(tokens, 2, axis=0)
    spread_cot = jnp.repeat(cotangent, 2, axis=0)

    def per_expert(carry, expert):
        back_acc, pair_acc = carry
        chosen = assigned == expert
        target = jnp.where(chosen, slots, rows_all).astype(jnp.int32)
        tok_rows = jnp.zeros((rows_all, D), jnp.bfloat16).at[target].set(spread_tok, mode='drop')
        cot_rows = jnp.zeros((rows_all, D), jnp.bfloat16).at[target].set(spread_cot, mode='drop')
        gate_mat = gate_weight[expert]
        up_mat = up_weight[expert]
        down_mat = down_weight[expert]
        gate_pre = jnp.dot(tok_rows, gate_mat, preferred_element_type=jnp.float32)
        up_pre = jnp.dot(tok_rows, up_mat, preferred_element_type=jnp.float32)
        back_hidden = jnp.dot(cot_rows, down_mat.T, preferred_element_type=jnp.float32)
        sig = jax.nn.sigmoid(gate_pre)
        pair_rows = lax.optimization_barrier(jnp.sum(back_hidden * gate_pre * sig * up_pre, axis=1))
        gate_grad = (back_hidden * up_pre * sig * (1.0 + gate_pre * (1.0 - sig))).astype(jnp.bfloat16)
        up_grad = (back_hidden * gate_pre * sig).astype(jnp.bfloat16)
        back_rows = jnp.dot(gate_grad, gate_mat.T, preferred_element_type=jnp.float32) + jnp.dot(up_grad, up_mat.T, preferred_element_type=jnp.float32)
        safe = jnp.where(chosen, slots, 0).astype(jnp.int32)
        back_acc = back_acc + jnp.where(chosen[:, None], back_rows[safe], jnp.float32(0.0))
        pair_acc = pair_acc + jnp.where(chosen, pair_rows[safe], jnp.float32(0.0))
        return ((back_acc, pair_acc), None)
    start = (jnp.zeros((TOKENS * 2, D), jnp.float32), jnp.zeros((TOKENS * 2,), jnp.float32))
    (back_acc, pair_acc), _ = lax.scan(per_expert, start, jnp.arange(EXPERTS, dtype=jnp.int32))
    back_tok = back_acc.reshape(TOKENS, 2, D)
    pair_tok = pair_acc.reshape(TOKENS, 2)
    token_grads = (mix[:, 0:1] * back_tok[:, 0] + mix[:, 1:2] * back_tok[:, 1]).astype(jnp.bfloat16)
    mean_dot = mix[:, 0:1] * pair_tok[:, 0:1] + mix[:, 1:2] * pair_tok[:, 1:2]
    logit_grads = mix * (pair_tok - mean_dot)
    loss_sums, query_grads, doc_grads = lax.map(one_group, (query_states, query_len, doc_states, doc_len, query_pos))
    loss = jnp.sum(loss_sums) / jnp.float32(GROUPS * GQ)
    return (token_grads, logit_grads, query_grads, doc_grads, loss)
```

```python
import math

import jax
import jax.numpy as jnp
from jax import lax
from jax.sharding import PartitionSpec as P

RING_Y = 4
CORES = 2
PAD = 128


def contract_last(left, right):
    return lax.dot_general(
        left, right, (((1,), (1,)), ((), ())), preferred_element_type=jnp.float32
    )


def pooled(states, lengths):
    positions = jnp.arange(states.shape[1], dtype=jnp.int32)
    valid = (positions[None, :] < lengths[:, None]).astype(jnp.bfloat16)
    summed = jnp.einsum("qt,qtd->qd", valid, states, preferred_element_type=jnp.float32)
    embedded = (summed / lengths[:, None].astype(jnp.float32)).astype(jnp.bfloat16)
    return (embedded, valid.astype(jnp.float32))


def split_high_low(values):
    high = values.astype(jnp.bfloat16)
    low = (values - high.astype(jnp.float32)).astype(jnp.bfloat16)
    return high, low


def shift_y(block, step):
    count = lax.axis_size("dp")
    pairs = [
        (i, i // RING_Y * RING_Y + (i % RING_Y + step) % RING_Y) for i in range(count)
    ]
    return lax.ppermute(block, "dp", pairs)


def shift_x(block, step):
    count = lax.axis_size("expert")
    pairs = [(i, (i + step * CORES) % count) for i in range(count)]
    return lax.ppermute(block, "expert", pairs)


def swap_core(block):
    count = lax.axis_size("expert")
    return lax.ppermute(block, "expert", [(i, i ^ 1) for i in range(count)])


def exchange_z(blocks):
    count = lax.axis_size("dp")
    groups = [list(range(y, count, RING_Y)) for y in range(RING_Y)]
    return lax.all_to_all(blocks, "dp", 0, 0, tiled=True, axis_index_groups=groups)


def pair_columns(first, second):
    rows = first.shape[0]
    columns = [*split_high_low(first), *split_high_low(second)]
    return jnp.concatenate(
        [c[:, None] for c in columns] + [jnp.zeros((rows, PAD - 4), jnp.bfloat16)], axis=1
    )


def pair_values(extra):
    wide = extra[:, :4].astype(jnp.float32)
    return wide[:, 0] + wide[:, 1], wide[:, 2] + wide[:, 3]


def add_partials(parts):
    width = parts[0].shape[1] - PAD
    total = sum(p[:, :width].astype(jnp.float32) for p in parts)
    pairs = [pair_values(p[:, width:]) for p in parts]
    return total, sum(p[0] for p in pairs), sum(p[1] for p in pairs)


def packed(total, first, second):
    return jnp.concatenate([total.astype(jnp.bfloat16), pair_columns(first, second)], axis=1)


def expert_rows(block, experts):
    columns = block.shape[1]
    width = columns - PAD
    grouped = block.reshape(-1, 2, 4, columns)
    inputs = grouped[:, 0, :, :width].reshape(-1, width)
    cots = grouped[:, 1, :, :width].reshape(-1, width)
    meta = grouped[:, 0, :, width : width + 6].reshape(-1, 6).astype(jnp.float32)
    routes = [meta[:, 0], meta[:, 1]]
    mixing = [meta[:, 2] + meta[:, 3], meta[:, 4] + meta[:, 5]]
    total = jnp.float32(0)
    first = second = jnp.float32(0)
    for number, gate_mat, up_mat, down_mat in experts:
        taken = [route == number.astype(jnp.float32) for route in routes]
        weight = jnp.where(taken[0], mixing[0], jnp.where(taken[1], mixing[1], 0.0))[:, None]
        gate_pre = jnp.dot(inputs, gate_mat, preferred_element_type=jnp.float32)
        up_pre = jnp.dot(inputs, up_mat, preferred_element_type=jnp.float32)
        back_hidden = contract_last(cots, down_mat)
        sigmoid_gate = jax.nn.sigmoid(gate_pre)
        silu = gate_pre * sigmoid_gate
        dots = jnp.sum(back_hidden * silu * up_pre, axis=1)
        first = first + jnp.where(taken[0], dots, 0.0)
        second = second + jnp.where(taken[1], dots, 0.0)
        back = weight * back_hidden
        gate_grad = (
            back * up_pre * sigmoid_gate * (1.0 + gate_pre * (1.0 - sigmoid_gate))
        ).astype(jnp.bfloat16)
        up_grad = (back * silu).astype(jnp.bfloat16)
        total = total + contract_last(gate_grad, gate_mat) + contract_last(up_grad, up_mat)
    return packed(total, first, second)


def expert_layer(tokens, out_grad, token_flags, routes, route_logits, gate_mat, up_mat, down_mat):
    tok_count, width = tokens.shape
    mixing = jax.nn.softmax(route_logits, axis=-1)
    cotangent = jnp.where(token_flags[:, None] == 0, out_grad, jnp.zeros_like(out_grad))
    number = lax.axis_index("expert")
    experts = [
        (number, gate_mat, up_mat, down_mat),
        (number ^ 1, swap_core(gate_mat), swap_core(up_mat), swap_core(down_mat)),
    ]
    mix_first = split_high_low(mixing[:, 0:1])
    mix_second = split_high_low(mixing[:, 1:2])
    meta = jnp.concatenate(
        [
            routes.astype(jnp.bfloat16),
            *mix_first,
            *mix_second,
            jnp.zeros((tok_count, PAD - 6), jnp.bfloat16),
        ],
        axis=1,
    )
    payload = jnp.concatenate(
        [
            jnp.concatenate([tokens, meta], axis=1),
            jnp.concatenate([cotangent, jnp.zeros_like(meta)], axis=1),
        ],
        axis=0,
    )
    ring_z = lax.axis_size("dp") // RING_Y
    column = exchange_z(jnp.broadcast_to(payload[None], (ring_z, *payload.shape)))
    half_z = ring_z // 2
    columns = width + PAD
    along = column[:half_z].reshape(-1, columns)
    across = column[half_z:].reshape(-1, columns)
    along = jnp.concatenate([along] + [shift_x(along, d) for d in (1, 2, -1)], axis=0)
    across = jnp.concatenate([across] + [shift_y(across, d) for d in (1, 2, -1)], axis=0)
    half = along.shape[0] // 2
    along_next, across_next = shift_y(along, 1), shift_x(across, 1)
    along_prev, across_prev = shift_y(along, -1), shift_x(across, -1)
    along_far = jnp.concatenate(
        [shift_y(along_next[:half], 1), shift_y(along_prev[half:], -1)], axis=0
    )
    across_far = jnp.concatenate(
        [shift_x(across_next[:half], 1), shift_x(across_prev[half:], -1)], axis=0
    )
    rows = half

    def both(left, right):
        out = expert_rows(jnp.concatenate([left, right], axis=0), experts)
        return out[:rows], out[rows:]

    along_own, across_own = both(along, across)
    along_next, across_next = both(along_next, across_next)
    along_prev, across_prev = both(along_prev, across_prev)
    along_far, across_far = both(along_far, across_far)
    along_sum = add_partials(
        [
            along_own,
            shift_y(along_next, -1),
            shift_y(along_prev, 1),
            shift_y(along_far, 2),
        ]
    )
    across_sum = add_partials(
        [
            across_own,
            shift_x(across_next, -1),
            shift_x(across_prev, 1),
            shift_x(across_far, 2),
        ]
    )
    along_sum, across_sum = packed(*along_sum), packed(*across_sum)
    quarter = rows // 4
    along_parts = [along_sum[i * quarter : (i + 1) * quarter] for i in range(4)]
    across_parts = [across_sum[i * quarter : (i + 1) * quarter] for i in range(4)]
    along_sum = add_partials(
        [along_parts[0]]
        + [shift_x(along_parts[i], -d) for i, d in ((1, 1), (2, 2), (3, -1))]
    )
    across_sum = add_partials(
        [across_parts[0]]
        + [shift_y(across_parts[i], -d) for i, d in ((1, 1), (2, 2), (3, -1))]
    )
    column = jnp.concatenate([packed(*along_sum), packed(*across_sum)], axis=0)
    column = exchange_z(column.reshape(ring_z, tok_count, columns))
    total, first, second = add_partials([column[i] for i in range(ring_z)])
    pair_tok = jnp.stack([first, second], axis=1)
    mean_dot = jnp.sum(mixing * pair_tok, axis=1, keepdims=True)
    return total.astype(jnp.bfloat16), mixing * (pair_tok - mean_dot)


def contrastive(query_states, query_len, doc_states, doc_len, query_pos):
    width = query_states.shape[-1]
    scale_factor = 1.0 / (0.02 * math.sqrt(width))
    query_emb, query_valid = pooled(query_states, query_len)
    doc_emb, doc_valid = pooled(doc_states, doc_len)
    own = query_emb.shape[0]
    members = lax.axis_size("dp")
    positives = jnp.concatenate(
        [
            query_pos[:, None].astype(jnp.bfloat16),
            jnp.zeros((own, PAD - 1), jnp.bfloat16),
        ],
        axis=1,
    )
    rows = jnp.concatenate(
        [
            jnp.concatenate([query_emb, positives], axis=1),
            jnp.concatenate([doc_emb, jnp.zeros_like(positives)], axis=1),
        ],
        axis=0,
    )
    everything = lax.all_gather(rows, "dp", axis=0, tiled=True)
    embeddings = everything[:, :width]
    count = 2 * own * members
    order = jnp.arange(count, dtype=jnp.int32)
    is_query = order % (2 * own) < own
    positive = everything[:, width].astype(jnp.float32).astype(jnp.int32)
    target_row = positive // own * (2 * own) + own + positive % own
    scores = contract_last(embeddings, embeddings) * scale_factor
    among = jnp.where(is_query[None, :], -jnp.inf, scores)
    highest = jnp.max(among, axis=1, keepdims=True)
    expo = jnp.exp(among - highest)
    totals = jnp.sum(expo, axis=1, keepdims=True)
    targets = order[None, :] == target_row[:, None]
    lse = highest[:, 0] + jnp.log(totals[:, 0])
    reached = jnp.sum(jnp.where(targets, scores, 0.0), axis=1)
    group_loss = jnp.sum(jnp.where(is_query, lse - reached, 0.0))
    coef = (expo / totals - targets.astype(jnp.float32)).astype(jnp.bfloat16)
    coef = jnp.where(is_query[:, None], coef, jnp.zeros_like(coef))
    start = lax.axis_index("dp") * (2 * own)
    mine = lax.dynamic_slice_in_dim(coef, start, 2 * own, axis=0)
    mine = mine + lax.dynamic_slice_in_dim(coef, start, 2 * own, axis=1).T
    grads = jnp.dot(mine, embeddings, preferred_element_type=jnp.float32) * scale_factor
    losses = lax.all_gather(jnp.broadcast_to(group_loss, (1, PAD)), "expert", axis=0, tiled=True)
    loss = jnp.sum(losses[:, 0]) / jnp.float32(own * members * lax.axis_size("expert"))
    query_grads = (
        (grads[:own] / query_len[:, None].astype(jnp.float32))[:, None, :]
        * query_valid[:, :, None]
    ).astype(jnp.bfloat16)
    doc_grads = (
        (grads[own:] / doc_len[:, None].astype(jnp.float32))[:, None, :] * doc_valid[:, :, None]
    ).astype(jnp.bfloat16)
    return query_grads, doc_grads, loss


def shards(
    tokens,
    out_grad,
    token_flags,
    routes,
    route_logits,
    gate_weight,
    up_weight,
    down_weight,
    query_states,
    query_len,
    doc_states,
    doc_len,
    query_pos,
):
    query_grads, doc_grads, loss = contrastive(
        query_states[0], query_len[0], doc_states[0], doc_len[0], query_pos[0]
    )
    token_grads, logit_grads = expert_layer(
        tokens,
        out_grad,
        token_flags,
        routes,
        route_logits,
        gate_weight[0],
        up_weight[0],
        down_weight[0],
    )
    return (token_grads, logit_grads, query_grads[None], doc_grads[None], loss)


def solution(mesh):
    placed = (
        P(("dp", "expert"), None),
        P(("dp", "expert"), None),
        P(("dp", "expert")),
        P(("dp", "expert"), None),
        P(("dp", "expert"), None),
        P("expert", None, "dp"),
        P("expert", None, "dp"),
        P("expert", "dp", None),
        P("expert", "dp", None, None),
        P("expert", "dp"),
        P("expert", "dp", None, None),
        P("expert", "dp"),
        P("expert", "dp"),
    )
    return jax.shard_map(
        shards,
        mesh=mesh,
        in_specs=placed,
        out_specs=(
            P(("dp", "expert"), None),
            P(("dp", "expert"), None),
            P("expert", "dp", None, None),
            P("expert", "dp", None, None),
            P(),
        ),
        check_vma=False,
    )
```

```python
import math

import jax
import jax.numpy as jnp
from jax import lax
from jax.experimental import pallas as pl
from jax.experimental.pallas import tpu as pltpu
from jax.sharding import PartitionSpec as P

RING_Y = 4
RING_X = 4
CORES = 2
PAD = 128
VMEM_BYTES = 48 * 1024 * 1024


def contract_last(left, right):
    return lax.dot_general(
        left, right, (((1,), (1,)), ((), ())), preferred_element_type=jnp.float32
    )


def pooled(states, lengths):
    positions = jnp.arange(states.shape[1], dtype=jnp.int32)
    valid = (positions[None, :] < lengths[:, None]).astype(jnp.bfloat16)
    summed = jnp.einsum("qt,qtd->qd", valid, states, preferred_element_type=jnp.float32)
    embedded = (summed / lengths[:, None].astype(jnp.float32)).astype(jnp.bfloat16)
    return (embedded, valid.astype(jnp.float32))


def shift_y(block, step):
    count = lax.axis_size("dp")
    pairs = [
        (i, i // RING_Y * RING_Y + (i % RING_Y + step) % RING_Y) for i in range(count)
    ]
    return lax.ppermute(block, "dp", pairs)


def shift_x(block, step):
    count = lax.axis_size("expert")
    pairs = [(i, (i + step * CORES) % count) for i in range(count)]
    return lax.ppermute(block, "expert", pairs)


def swap_core(block):
    count = lax.axis_size("expert")
    return lax.ppermute(block, "expert", [(i, i ^ 1) for i in range(count)])


def exchange_x(blocks):
    count = lax.axis_size("expert")
    groups = [list(range(c, count, CORES)) for c in range(CORES)]
    return lax.all_to_all(blocks, "expert", 0, 0, tiled=True, axis_index_groups=groups)


def exchange_z(blocks):
    count = lax.axis_size("dp")
    groups = [list(range(y, count, RING_Y)) for y in range(RING_Y)]
    return lax.all_to_all(blocks, "dp", 0, 0, tiled=True, axis_index_groups=groups)


def in_vmem(count):
    return [pl.BlockSpec(memory_space=pltpu.VMEM)] * count


def in_hbm(count):
    return [pl.BlockSpec(memory_space=pltpu.HBM)] * count


def high_low(values):
    high = values.astype(jnp.bfloat16).astype(jnp.float32)
    return high, values - high


def at_lanes(rows, columns):
    lane = lax.broadcasted_iota(jnp.int32, (rows, PAD), 1)
    placed = jnp.zeros((rows, PAD), jnp.float32)
    for i, column in enumerate(columns):
        placed = jnp.where(lane == i, column, placed)
    return placed


def payload_kernel(tok_ref, cot_ref, meta_ref, out_ref, held):
    tok_count, width = tok_ref.shape
    meta = meta_ref[...]
    held[:tok_count, :width] = tok_ref[...].astype(jnp.float32)
    held[tok_count:, :width] = jnp.where(
        meta[:, 6:7] == 0, cot_ref[...].astype(jnp.float32), 0.0
    )
    held[:tok_count, width:] = meta
    held[tok_count:, width:] = jnp.zeros((tok_count, PAD), jnp.float32)
    rows = held[...].astype(jnp.bfloat16)
    for i in range(out_ref.shape[0]):
        out_ref[i] = rows


def softmax_of_two(logits):
    first, second = logits[:, 0:1], logits[:, 1:2]
    top = jnp.maximum(first, second)
    first, second = jnp.exp(first - top), jnp.exp(second - top)
    return first / (first + second), second / (first + second)


def build_payload(tokens, out_grad, token_flags, routes, route_logits, copies):
    tok_count, width = tokens.shape
    first, second = softmax_of_two(route_logits)
    meta = at_lanes(
        tok_count,
        [
            routes[:, 0:1].astype(jnp.float32),
            routes[:, 1:2].astype(jnp.float32),
            *high_low(first),
            *high_low(second),
            token_flags[:, None].astype(jnp.float32),
        ],
    )
    return pl.pallas_call(
        payload_kernel,
        out_shape=jax.ShapeDtypeStruct((copies, 2 * tok_count, width + PAD), jnp.bfloat16),
        in_specs=in_vmem(3),
        out_specs=in_vmem(1)[0],
        scratch_shapes=[pltpu.VMEM((2 * tok_count, width + PAD), jnp.float32)],
        compiler_params=pltpu.CompilerParams(vmem_limit_bytes=VMEM_BYTES),
    )(tokens, out_grad, meta)


def expert_kernel(count, merged, number_ref, *refs):
    blocks, refs = refs[:count], refs[count:]
    weights, refs = refs[:6], refs[6:]
    outs, refs = refs[: count // merged], refs[count // merged :]
    held, (sources, inputs, cots, results, in_sems, sems, out_sems) = refs[:6], refs[6:]
    loads = [
        pltpu.make_async_copy(block, sources.at[i], in_sems.at[i])
        for i, block in enumerate(blocks)
    ]
    copies = [
        pltpu.make_async_copy(src, dst, sems.at[i])
        for i, (src, dst) in enumerate(zip(weights, held))
    ]
    for copy in loads + copies:
        copy.start()
    total_rows, columns = blocks[0].shape
    width = columns - PAD
    rows = total_rows // 2
    row = lax.broadcasted_iota(jnp.int32, (rows, total_rows), 0)
    source = lax.broadcasted_iota(jnp.int32, (rows, total_rows), 1)
    place = row // 4 * 8 + row % 4
    pick_tok = (source == place).astype(jnp.bfloat16)
    pick_cot = (source == place + 4).astype(jnp.bfloat16)
    metas = []
    for i, load in enumerate(loads):
        own = slice(i * rows, (i + 1) * rows)
        load.wait()
        block = sources.at[i]
        inputs[own, :] = jnp.dot(
            pick_tok, block[:, :width], preferred_element_type=jnp.float32
        ).astype(jnp.bfloat16)
        cots[own, :] = jnp.dot(
            pick_cot, block[:, :width], preferred_element_type=jnp.float32
        ).astype(jnp.bfloat16)
        metas.append(
            jnp.dot(pick_tok, block[:, width:], preferred_element_type=jnp.float32)
        )
    meta = jnp.concatenate(metas, axis=0)
    routes = [meta[:, 0:1], meta[:, 1:2]]
    mixing = [meta[:, 2:3] + meta[:, 3:4], meta[:, 4:5] + meta[:, 5:6]]
    number = number_ref[0]
    pairs = [jnp.zeros_like(routes[0]), jnp.zeros_like(routes[0])]
    factors = []
    for e in range(2):
        expert = (number ^ e).astype(jnp.float32)
        taken = [route == expert for route in routes]
        weight = jnp.where(taken[0], mixing[0], jnp.where(taken[1], mixing[1], 0.0))
        gate_mat, up_mat, down_mat = held[3 * e : 3 * e + 3]
        copies[3 * e].wait()
        gate_pre = jnp.dot(inputs[...], gate_mat[...], preferred_element_type=jnp.float32)
        copies[3 * e + 1].wait()
        up_pre = jnp.dot(inputs[...], up_mat[...], preferred_element_type=jnp.float32)
        copies[3 * e + 2].wait()
        back_hidden = contract_last(cots[...], down_mat[...])
        sigmoid_gate = jax.nn.sigmoid(gate_pre)
        silu = gate_pre * sigmoid_gate
        dots = jnp.sum(back_hidden * silu * up_pre, axis=1, keepdims=True)
        pairs = [p + jnp.where(t, dots, 0.0) for p, t in zip(pairs, taken)]
        back = weight * back_hidden
        gate_grad = back * up_pre * sigmoid_gate * (1.0 + gate_pre * (1.0 - sigmoid_gate))
        factors.append((gate_grad.astype(jnp.bfloat16), gate_mat))
        factors.append(((back * silu).astype(jnp.bfloat16), up_mat))
    step = min(width, 512)
    each = merged * rows
    stores = []

    def store(low, size):
        for i, out in enumerate(outs):
            copy = pltpu.make_async_copy(
                results.at[pl.ds(i * each, each), pl.ds(low, size)],
                out.at[:, pl.ds(low, size)],
                out_sems.at[low // step, i],
            )
            copy.start()
            stores.append(copy)

    extra = at_lanes(count * rows, [*high_low(pairs[0]), *high_low(pairs[1])])
    results[:, width:] = extra.astype(jnp.bfloat16)
    store(width, PAD)
    for low in range(0, width, step):
        part = sum(contract_last(g, mat[low : low + step, :]) for g, mat in factors)
        results[:, low : low + step] = part.astype(jnp.bfloat16)
        store(low, step)
    for copy in stores:
        copy.wait()


def expert_rows(blocks, number, weights, merged=1):
    count = len(blocks)
    total_rows, columns = blocks[0].shape
    rows, width = total_rows // 2, columns - PAD
    hidden = weights[0].shape[1]
    return pl.pallas_call(
        lambda *refs: expert_kernel(count, merged, *refs),
        out_shape=[jax.ShapeDtypeStruct((merged * rows, columns), jnp.bfloat16)]
        * (count // merged),
        in_specs=[
            pl.BlockSpec(memory_space=pltpu.SMEM),
            *in_hbm(count + 6),
        ],
        out_specs=in_hbm(count // merged),
        scratch_shapes=[
            *[pltpu.VMEM(w.shape, jnp.bfloat16) for w in weights],
            pltpu.VMEM((count, total_rows, columns), jnp.bfloat16),
            pltpu.VMEM((count * rows, width), jnp.bfloat16),
            pltpu.VMEM((count * rows, width), jnp.bfloat16),
            pltpu.VMEM((count * rows, columns), jnp.bfloat16),
            pltpu.SemaphoreType.DMA((count,)),
            pltpu.SemaphoreType.DMA((6,)),
            pltpu.SemaphoreType.DMA((width // min(width, 512) + 1, count // merged)),
        ],
        compiler_params=pltpu.CompilerParams(vmem_limit_bytes=VMEM_BYTES),
        cost_estimate=pl.CostEstimate(
            flops=20 * count * rows * width * hidden,
            bytes_accessed=12 * width * hidden + 6 * count * rows * columns,
            transcendentals=2 * count * rows * hidden,
        ),
    )(number, *blocks, *weights)


def add_kernel(count, *refs):
    outs = refs[-(len(refs) // (count + 1)) :]
    width = outs[0].shape[1] - PAD
    for i, out in enumerate(outs):
        parts = refs[i * count : (i + 1) * count]
        total = parts[0][:, :width].astype(jnp.float32)
        extra = parts[0][:, width:].astype(jnp.float32)
        for part in parts[1:]:
            total += part[:, :width].astype(jnp.float32)
            extra += part[:, width:].astype(jnp.float32)
        out[:, :width] = total.astype(jnp.bfloat16)
        values = extra + pltpu.roll(extra, PAD - 1, 1)
        high = values.astype(jnp.bfloat16).astype(jnp.float32)
        low = pltpu.roll(values - high, 1, 1)
        lane = lax.broadcasted_iota(jnp.int32, extra.shape, 1)
        kept = jnp.where(lane % 2 == 0, high, low)
        out[:, width:] = jnp.where(lane < 4, kept, 0.0).astype(jnp.bfloat16)


def add_partials(*groups):
    count = len(groups[0])
    return pl.pallas_call(
        lambda *refs: add_kernel(count, *refs),
        out_shape=[jax.ShapeDtypeStruct(g[0].shape, jnp.bfloat16) for g in groups],
        in_specs=in_vmem(count * len(groups)),
        out_specs=in_vmem(len(groups)),
        compiler_params=pltpu.CompilerParams(vmem_limit_bytes=VMEM_BYTES),
        cost_estimate=pl.CostEstimate(
            flops=count * sum(g[0].size for g in groups),
            bytes_accessed=2 * (count + 1) * sum(g[0].size for g in groups),
            transcendentals=0,
        ),
    )(*[p for g in groups for p in g])


def halves_kernel(*refs):
    *refs, held, in_sems, out_sems = refs
    count = len(refs) // 2
    half = refs[count].shape[0]
    loads = [
        pltpu.make_async_copy(src.at[pl.ds(i % 2 * half, half)], held.at[i], in_sems.at[i])
        for i, src in enumerate(refs[:count])
    ]
    stores = [
        pltpu.make_async_copy(held.at[i], dst, out_sems.at[i])
        for i, dst in enumerate(refs[count:])
    ]
    for load in loads:
        load.start()
    for load, store in zip(loads, stores):
        load.wait()
        store.start()
    for store in stores:
        store.wait()


def first_and_last_halves(blocks):
    rows, columns = blocks[0].shape
    count, half = len(blocks), rows // 2
    return pl.pallas_call(
        halves_kernel,
        out_shape=[jax.ShapeDtypeStruct((half, columns), b.dtype) for b in blocks],
        in_specs=in_hbm(count),
        out_specs=in_hbm(count),
        scratch_shapes=[
            pltpu.VMEM((count, half, columns), blocks[0].dtype),
            pltpu.SemaphoreType.DMA((count,)),
            pltpu.SemaphoreType.DMA((count,)),
        ],
        compiler_params=pltpu.CompilerParams(vmem_limit_bytes=VMEM_BYTES),
    )(*blocks)


def expert_layer(
    tokens, out_grad, token_flags, routes, route_logits, gate_mat, up_mat, down_mat, group
):
    tok_count, width = tokens.shape
    columns = width + PAD
    ring_z = lax.axis_size("dp") // RING_Y
    number = lax.axis_index("expert").astype(jnp.int32).reshape(1)
    weights = [gate_mat, up_mat, down_mat]
    swapped = [swap_core(w) for w in weights]
    payload = build_payload(tokens, out_grad, token_flags, routes, route_logits, ring_z)
    column, swapped = lax.optimization_barrier((exchange_z(payload), swapped))
    weights += swapped
    half_z = ring_z // 2
    along = column[:half_z].reshape(-1, columns)
    across = column[half_z:].reshape(-1, columns)
    along = exchange_x(jnp.broadcast_to(along, (RING_X, *along.shape))).reshape(-1, columns)
    across = jnp.concatenate([across] + [shift_y(across, d) for d in (1, 2, -1)], axis=0)
    near_in = [shift_y(along, 1), shift_y(along, -1), shift_x(across, 1), shift_x(across, -1)]
    along_own, across_own = expert_rows([along, across], number, weights)
    halves = first_and_last_halves(near_in)
    halves, along_own, across_own = lax.optimization_barrier((halves, along_own, across_own))
    far_in = [
        shift_y(halves[0], 1),
        shift_y(halves[1], -1),
        shift_x(halves[2], 1),
        shift_x(halves[3], -1),
    ]
    near = expert_rows(near_in, number, weights)
    far_in, near, group = lax.optimization_barrier((far_in, near, group))
    far = expert_rows(far_in, number, weights, merged=2)
    near = [shift_y(near[0], -1), shift_y(near[1], 1), shift_x(near[2], -1), shift_x(near[3], 1)]
    far, near = lax.optimization_barrier((far, near))
    far = [shift_y(far[0], 2), shift_x(far[1], 2)]
    along_sum, across_sum = add_partials(
        [along_own, near[0], near[1], far[0]], [across_own, near[2], near[3], far[1]]
    )
    quarter = along_sum.shape[0] // 4
    along_parts = exchange_x(along_sum.reshape(RING_X, quarter, columns))
    across_parts = [across_sum[i * quarter : (i + 1) * quarter] for i in range(4)]
    steps = (1, 2, -1)
    along_sum, across_sum = add_partials(
        [along_parts[i] for i in range(4)],
        [across_parts[0]] + [shift_y(b, -d) for b, d in zip(across_parts[1:], steps)],
    )
    column = jnp.concatenate([along_sum, across_sum], axis=0)
    column = exchange_z(column.reshape(ring_z, tok_count, columns))
    total = jnp.sum(column.astype(jnp.float32), axis=0)
    pair_tok = total[:, width : width + 4].reshape(tok_count, 2, 2).sum(axis=2)
    mixing = jax.nn.softmax(route_logits, axis=-1)
    mean_dot = jnp.sum(mixing * pair_tok, axis=1, keepdims=True)
    return total[:, :width].astype(jnp.bfloat16), mixing * (pair_tok - mean_dot), contrast(*group)


def gather_group(query_states, query_len, doc_states, doc_len, query_pos):
    query_emb, query_valid = pooled(query_states, query_len)
    doc_emb, doc_valid = pooled(doc_states, doc_len)
    own = query_emb.shape[0]
    positives = jnp.concatenate(
        [
            query_pos[:, None].astype(jnp.bfloat16),
            jnp.zeros((own, PAD - 1), jnp.bfloat16),
        ],
        axis=1,
    )
    rows = jnp.concatenate(
        [
            jnp.concatenate([query_emb, positives], axis=1),
            jnp.concatenate([doc_emb, jnp.zeros_like(positives)], axis=1),
        ],
        axis=0,
    )
    everything = lax.all_gather(rows, "dp", axis=0, tiled=True)
    return everything, query_valid, doc_valid, query_len, doc_len


def contrast(everything, query_valid, doc_valid, query_len, doc_len):
    width = everything.shape[1] - PAD
    own = query_len.shape[0]
    members = lax.axis_size("dp")
    scale_factor = 1.0 / (0.02 * math.sqrt(width))
    embeddings = everything[:, :width]
    count = 2 * own * members
    order = jnp.arange(count, dtype=jnp.int32)
    is_query = order % (2 * own) < own
    positive = everything[:, width].astype(jnp.float32).astype(jnp.int32)
    target_row = positive // own * (2 * own) + own + positive % own
    scores = contract_last(embeddings, embeddings) * scale_factor
    among = jnp.where(is_query[None, :], -jnp.inf, scores)
    highest = jnp.max(among, axis=1, keepdims=True)
    expo = jnp.exp(among - highest)
    totals = jnp.sum(expo, axis=1, keepdims=True)
    targets = order[None, :] == target_row[:, None]
    lse = highest[:, 0] + jnp.log(totals[:, 0])
    reached = jnp.sum(jnp.where(targets, scores, 0.0), axis=1)
    group_loss = jnp.sum(jnp.where(is_query, lse - reached, 0.0))
    coef = (expo / totals - targets.astype(jnp.float32)).astype(jnp.bfloat16)
    coef = jnp.where(is_query[:, None], coef, jnp.zeros_like(coef))
    start = lax.axis_index("dp") * (2 * own)
    mine = lax.dynamic_slice_in_dim(coef, start, 2 * own, axis=0)
    mine = mine + lax.dynamic_slice_in_dim(coef, start, 2 * own, axis=1).T
    grads = jnp.dot(mine, embeddings, preferred_element_type=jnp.float32) * scale_factor
    query_grads = (
        (grads[:own] / query_len[:, None].astype(jnp.float32))[:, None, :]
        * query_valid[:, :, None]
    ).astype(jnp.bfloat16)
    doc_grads = (
        (grads[own:] / doc_len[:, None].astype(jnp.float32))[:, None, :] * doc_valid[:, :, None]
    ).astype(jnp.bfloat16)
    return query_grads, doc_grads, group_loss


def shards(
    tokens,
    out_grad,
    token_flags,
    routes,
    route_logits,
    gate_weight,
    up_weight,
    down_weight,
    query_states,
    query_len,
    doc_states,
    doc_len,
    query_pos,
):
    group = gather_group(
        query_states[0], query_len[0], doc_states[0], doc_len[0], query_pos[0]
    )
    token_grads, logit_grads, side = expert_layer(
        tokens,
        out_grad,
        token_flags,
        routes,
        route_logits,
        gate_weight[0],
        up_weight[0],
        down_weight[0],
        group,
    )
    query_grads, doc_grads, group_loss = side
    experts = lax.axis_size("expert")
    losses = lax.all_to_all(
        jnp.broadcast_to(group_loss, (experts, PAD)), "expert", 0, 0, tiled=True
    )
    queries = query_pos.shape[1] * lax.axis_size("dp") * experts
    loss = jnp.sum(losses[:, 0]) / jnp.float32(queries)
    return (token_grads, logit_grads, query_grads[None], doc_grads[None], loss)


def solution(mesh):
    placed = (
        P(("dp", "expert"), None),
        P(("dp", "expert"), None),
        P(("dp", "expert")),
        P(("dp", "expert"), None),
        P(("dp", "expert"), None),
        P("expert", None, "dp"),
        P("expert", None, "dp"),
        P("expert", "dp", None),
        P("expert", "dp", None, None),
        P("expert", "dp"),
        P("expert", "dp", None, None),
        P("expert", "dp"),
        P("expert", "dp"),
    )
    return jax.shard_map(
        shards,
        mesh=mesh,
        in_specs=placed,
        out_specs=(
            P(("dp", "expert"), None),
            P(("dp", "expert"), None),
            P("expert", "dp", None, None),
            P("expert", "dp", None, None),
            P(),
        ),
        check_vma=False,
    )
```

```python
import math

import jax
import jax.numpy as jnp
from jax import lax
from jax.experimental import pallas as pl
from jax.experimental.pallas import tpu as pltpu
from jax.sharding import PartitionSpec as P

RING_Y = 4
CORES = 2
PAD = 128
VMEM_BYTES = 32 * 1024 * 1024


def contract_last(left, right):
    return lax.dot_general(
        left, right, (((1,), (1,)), ((), ())), preferred_element_type=jnp.float32
    )


def pooled(states, lengths):
    positions = jnp.arange(states.shape[1], dtype=jnp.int32)
    valid = (positions[None, :] < lengths[:, None]).astype(jnp.bfloat16)
    summed = jnp.einsum("qt,qtd->qd", valid, states, preferred_element_type=jnp.float32)
    return (summed / lengths[:, None].astype(jnp.float32)).astype(jnp.bfloat16)


def shift_y(block, step):
    count = lax.axis_size("dp")
    pairs = [
        (i, i // RING_Y * RING_Y + (i % RING_Y + step) % RING_Y) for i in range(count)
    ]
    return lax.ppermute(block, "dp", pairs)


def shift_x(block, step):
    count = lax.axis_size("expert")
    pairs = [(i, (i + step * CORES) % count) for i in range(count)]
    return lax.ppermute(block, "expert", pairs)


def shift_outward(block, axis, step):
    expert_count, count = lax.axis_size("expert"), lax.axis_size("dp")
    pairs = []
    for i in range(count):
        for e in range(expert_count):
            z, y, x, core = i // RING_Y, i % RING_Y, e // CORES, e % CORES
            move = step if core == 0 else -step
            if axis == "z":
                z = (z + move) % (count // RING_Y)
            elif axis == "y":
                y = (y + move) % RING_Y
            else:
                x = (x + move) % (expert_count // CORES)
            target = (z * RING_Y + y) * expert_count + x * CORES + core
            pairs.append((i * expert_count + e, target))
    return lax.ppermute(block, ("dp", "expert"), pairs)


def swap_core(block):
    count = lax.axis_size("expert")
    return lax.ppermute(block, "expert", [(i, i ^ 1) for i in range(count)])


def exchange_z(blocks):
    count = lax.axis_size("dp")
    groups = [list(range(y, count, RING_Y)) for y in range(RING_Y)]
    return lax.all_to_all(blocks, "dp", 0, 0, tiled=True, axis_index_groups=groups)


def in_vmem(count):
    return [pl.BlockSpec(memory_space=pltpu.VMEM)] * count


def in_hbm(count):
    return [pl.BlockSpec(memory_space=pltpu.HBM)] * count


def from_hbm(arrays):
    return [pltpu.with_memory_space_constraint(a, pltpu.HBM) for a in arrays]


def high_low(values):
    high = values.astype(jnp.bfloat16).astype(jnp.float32)
    return high, values - high


def at_lanes(rows, columns):
    lane = lax.broadcasted_iota(jnp.int32, (rows, PAD), 1)
    placed = jnp.zeros((rows, PAD), jnp.float32)
    for i, column in enumerate(columns):
        placed = jnp.where(lane == i, column, placed)
    return placed


def payload_kernel(tok_ref, cot_ref, meta_ref, out_ref, held):
    tok_count, width = tok_ref.shape
    meta = meta_ref[...]
    held[:tok_count, :width] = tok_ref[...].astype(jnp.float32)
    held[tok_count:, :width] = jnp.where(
        meta[:, 6:7] == 0, cot_ref[...].astype(jnp.float32), 0.0
    )
    held[:tok_count, width:] = meta
    held[tok_count:, width:] = jnp.zeros((tok_count, PAD), jnp.float32)
    rows = held[...].astype(jnp.bfloat16)
    for i in range(out_ref.shape[0]):
        out_ref[i] = rows


def softmax_of_two(logits):
    first, second = logits[:, 0:1], logits[:, 1:2]
    top = jnp.maximum(first, second)
    first, second = jnp.exp(first - top), jnp.exp(second - top)
    return first / (first + second), second / (first + second)


def build_payload(tokens, out_grad, token_flags, routes, route_logits, copies):
    tok_count, width = tokens.shape
    first, second = softmax_of_two(route_logits)
    meta = at_lanes(
        tok_count,
        [
            routes[:, 0:1].astype(jnp.float32),
            routes[:, 1:2].astype(jnp.float32),
            *high_low(first),
            *high_low(second),
            token_flags[:, None].astype(jnp.float32),
        ],
    )
    return pl.pallas_call(
        payload_kernel,
        out_shape=jax.ShapeDtypeStruct((copies, 2 * tok_count, width + PAD), jnp.bfloat16),
        in_specs=in_vmem(3),
        out_specs=in_vmem(1)[0],
        scratch_shapes=[pltpu.VMEM((2 * tok_count, width + PAD), jnp.float32)],
        compiler_params=pltpu.CompilerParams(vmem_limit_bytes=VMEM_BYTES),
    )(tokens, out_grad, meta)


def expert_kernel(count, merged, number_ref, *refs):
    blocks, refs = refs[:count], refs[count:]
    weights, refs = refs[:6], refs[6:]
    outs, refs = refs[: count // merged], refs[count // merged :]
    sources, inputs, cots, results, in_sems, out_sems = refs
    total_rows, columns = blocks[0].shape
    width = columns - PAD
    rows = total_rows // 2
    loads = [
        pltpu.make_async_copy(
            block, sources.at[pl.ds(i * total_rows, total_rows)], in_sems.at[i]
        )
        for i, block in enumerate(blocks)
    ]
    for load in loads:
        load.start()
    group = min(256, count * total_rows)
    half = group // 2
    row = lax.broadcasted_iota(jnp.int32, (group, group), 0)
    source = lax.broadcasted_iota(jnp.int32, (group, group), 1)
    nth = row % half
    pick = (source == nth // 4 * 8 + nth % 4 + row // half * 4).astype(jnp.bfloat16)
    step = min(width, 512)
    metas = []
    for low in range(0, count * total_rows, group):
        for load in loads[low // total_rows : (low + group) // total_rows]:
            load.wait()
        own = slice(low // 2, low // 2 + half)
        for left in range(0, width, step):
            picked = jnp.dot(
                pick,
                sources[low : low + group, left : left + step],
                preferred_element_type=jnp.float32,
            ).astype(jnp.bfloat16)
            inputs[own, left : left + step] = picked[:half]
            cots[own, left : left + step] = picked[half:]
        metas.append(
            jnp.dot(
                pick, sources[low : low + group, width:], preferred_element_type=jnp.float32
            )[:half]
        )
    meta = jnp.concatenate(metas, axis=0)
    routes = [meta[:, 0:1], meta[:, 1:2]]
    mixing = [meta[:, 2:3] + meta[:, 3:4], meta[:, 4:5] + meta[:, 5:6]]
    number = number_ref[0]
    pairs = [jnp.zeros_like(routes[0]), jnp.zeros_like(routes[0])]
    factors = []
    for e in range(2):
        expert = (number ^ e).astype(jnp.float32)
        taken = [route == expert for route in routes]
        weight = jnp.where(taken[0], mixing[0], jnp.where(taken[1], mixing[1], 0.0))
        gate_mat, up_mat, down_mat = weights[3 * e : 3 * e + 3]
        gate_pre = jnp.dot(inputs[...], gate_mat[...], preferred_element_type=jnp.float32)
        up_pre = jnp.dot(inputs[...], up_mat[...], preferred_element_type=jnp.float32)
        back_hidden = contract_last(cots[...], down_mat[...])
        sigmoid_gate = jax.nn.sigmoid(gate_pre)
        silu = gate_pre * sigmoid_gate
        dots = jnp.sum(back_hidden * silu * up_pre, axis=1, keepdims=True)
        pairs = [p + jnp.where(t, dots, 0.0) for p, t in zip(pairs, taken)]
        back = weight * back_hidden
        gate_grad = back * up_pre * sigmoid_gate * (1.0 + gate_pre * (1.0 - sigmoid_gate))
        factors.append((gate_grad.astype(jnp.bfloat16), gate_mat))
        factors.append(((back * silu).astype(jnp.bfloat16), up_mat))
    each = merged * rows
    stores = []

    def store(low, size):
        for i, out in enumerate(outs):
            copy = pltpu.make_async_copy(
                results.at[pl.ds(i * each, each), pl.ds(low, size)],
                out.at[:, pl.ds(low, size)],
                out_sems.at[low // step, i],
            )
            copy.start()
            stores.append(copy)

    extra = at_lanes(count * rows, [*high_low(pairs[0]), *high_low(pairs[1])])
    results[:, width:] = extra.astype(jnp.bfloat16)
    store(width, PAD)
    for low in range(0, width, step):
        part = sum(contract_last(g, mat[low : low + step, :]) for g, mat in factors)
        results[:, low : low + step] = part.astype(jnp.bfloat16)
        store(low, step)
    for copy in stores:
        copy.wait()


def expert_rows(blocks, number, weights, merged=1):
    count = len(blocks)
    total_rows, columns = blocks[0].shape
    rows, width = total_rows // 2, columns - PAD
    hidden = weights[0].shape[1]
    return pl.pallas_call(
        lambda *refs: expert_kernel(count, merged, *refs),
        out_shape=[pltpu.HBM((merged * rows, columns), jnp.bfloat16)]
        * (count // merged),
        in_specs=[
            pl.BlockSpec(memory_space=pltpu.SMEM),
            *in_hbm(count),
            *in_vmem(6),
        ],
        out_specs=in_hbm(count // merged),
        scratch_shapes=[
            pltpu.VMEM((count * total_rows, columns), jnp.bfloat16),
            pltpu.VMEM((count * rows, width), jnp.bfloat16),
            pltpu.VMEM((count * rows, width), jnp.bfloat16),
            pltpu.VMEM((count * rows, columns), jnp.bfloat16),
            pltpu.SemaphoreType.DMA((count,)),
            pltpu.SemaphoreType.DMA((width // min(width, 512) + 1, count // merged)),
        ],
        compiler_params=pltpu.CompilerParams(vmem_limit_bytes=VMEM_BYTES),
        cost_estimate=pl.CostEstimate(
            flops=20 * count * rows * width * hidden,
            bytes_accessed=12 * width * hidden + 6 * count * rows * columns,
            transcendentals=2 * count * rows * hidden,
        ),
    )(number, *from_hbm(blocks), *weights)


def added(parts):
    width = parts[0].shape[1] - PAD
    total = parts[0][:, :width].astype(jnp.float32)
    extra = parts[0][:, width:].astype(jnp.float32)
    for part in parts[1:]:
        total += part[:, :width].astype(jnp.float32)
        extra += part[:, width:].astype(jnp.float32)
    values = extra + pltpu.roll(extra, PAD - 1, 1)
    high = values.astype(jnp.bfloat16).astype(jnp.float32)
    low = pltpu.roll(values - high, 1, 1)
    lane = lax.broadcasted_iota(jnp.int32, extra.shape, 1)
    kept = jnp.where(lane % 2 == 0, high, low)
    return total, jnp.where(lane < 4, kept, 0.0)


def load_all(refs, held, sems):
    copies = [
        pltpu.make_async_copy(ref, held.at[i], sems.at[i]) for i, ref in enumerate(refs)
    ]
    for copy in copies:
        copy.start()
    return copies


def add_kernel(count, pieces, *refs):
    *refs, held, results, in_sems, out_sems = refs
    groups = len(refs) // (count + pieces)
    outs = refs[count * groups :]
    loads = load_all(refs[: count * groups], held, in_sems)
    width = held.shape[2] - PAD
    size = held.shape[1] // pieces
    stores = []
    for i in range(groups):
        for load in loads[i * count : (i + 1) * count]:
            load.wait()
        total, extra = added([held.at[i * count + j] for j in range(count)])
        results[i, :, :width] = total.astype(jnp.bfloat16)
        results[i, :, width:] = extra.astype(jnp.bfloat16)
        for j, out in enumerate(outs[i * pieces : (i + 1) * pieces]):
            source = results.at[i, pl.ds(j * size, size)]
            store = pltpu.make_async_copy(source, out, out_sems.at[i, j])
            store.start()
            stores.append(store)
    for store in stores:
        store.wait()


def add_last_kernel(count, *refs):
    *refs, out, held, sems = refs
    loads = load_all(refs, held, sems)
    size, width = out.shape[1], out.shape[2] - PAD
    place = 0
    for low in range(0, len(refs), count):
        for load in loads[low : low + count]:
            load.wait()
        total, extra = added([held.at[low + j] for j in range(count)])
        for row in range(0, total.shape[0], size):
            out[place, :, :width] = total[row : row + size].astype(jnp.bfloat16)
            out[place, :, width:] = extra[row : row + size].astype(jnp.bfloat16)
            place += 1


def add_last(first, second, size):
    rows, columns = first[0].shape
    return pl.pallas_call(
        lambda *refs: add_last_kernel(len(first), *refs),
        out_shape=jax.ShapeDtypeStruct((2 * rows // size, size, columns), jnp.bfloat16),
        in_specs=in_hbm(2 * len(first)),
        out_specs=in_vmem(1)[0],
        scratch_shapes=[
            pltpu.VMEM((2 * len(first), rows, columns), jnp.bfloat16),
            pltpu.SemaphoreType.DMA((2 * len(first),)),
        ],
        compiler_params=pltpu.CompilerParams(vmem_limit_bytes=VMEM_BYTES),
    )(*from_hbm([*first, *second]))


def add_partials(groups, pieces=1):
    count, (rows, columns) = len(groups[0]), groups[0][0].shape
    size = len(groups) * rows * columns
    outs = pl.pallas_call(
        lambda *refs: add_kernel(count, pieces, *refs),
        out_shape=[pltpu.HBM((rows // pieces, columns), jnp.bfloat16)] * (len(groups) * pieces),
        in_specs=in_hbm(count * len(groups)),
        out_specs=in_hbm(len(groups) * pieces),
        scratch_shapes=[
            pltpu.VMEM((count * len(groups), rows, columns), jnp.bfloat16),
            pltpu.VMEM((len(groups), rows, columns), jnp.bfloat16),
            pltpu.SemaphoreType.DMA((count * len(groups),)),
            pltpu.SemaphoreType.DMA((len(groups), pieces)),
        ],
        compiler_params=pltpu.CompilerParams(vmem_limit_bytes=VMEM_BYTES),
        cost_estimate=pl.CostEstimate(
            flops=count * size, bytes_accessed=2 * (count + 1) * size, transcendentals=0
        ),
    )(*from_hbm([p for g in groups for p in g]))
    return [outs[i * pieces : (i + 1) * pieces] for i in range(len(groups))]


def stack_kernel(counts, *refs):
    *refs, sems = refs
    blocks, refs = refs[: sum(counts)], refs[sum(counts) :]
    outs, held = refs[: len(counts)], refs[len(counts) :]
    moves, place = [], 0
    for count, out, buffer in zip(counts, outs, held):
        low = 0
        for block in blocks[place : place + count]:
            here = buffer.at[pl.ds(low, block.shape[0])]
            there = out.at[pl.ds(low, block.shape[0])]
            moves.append(
                (
                    pltpu.make_async_copy(block, here, sems.at[0, len(moves)]),
                    pltpu.make_async_copy(here, there, sems.at[1, len(moves)]),
                )
            )
            low += block.shape[0]
        place += count
    for load, _ in moves:
        load.start()
    for load, store in moves:
        load.wait()
        store.start()
    for _, store in moves:
        store.wait()


def stack_rows(*groups):
    counts = [len(g) for g in groups]
    shapes = [(sum(b.shape[0] for b in g), g[0].shape[1]) for g in groups]
    return pl.pallas_call(
        lambda *refs: stack_kernel(counts, *refs),
        out_shape=[pltpu.HBM(s, jnp.bfloat16) for s in shapes],
        in_specs=in_hbm(sum(counts)),
        out_specs=in_hbm(len(groups)),
        scratch_shapes=[
            *[pltpu.VMEM(s, jnp.bfloat16) for s in shapes],
            pltpu.SemaphoreType.DMA((2, sum(counts))),
        ],
        compiler_params=pltpu.CompilerParams(vmem_limit_bytes=VMEM_BYTES),
    )(*from_hbm([b for g in groups for b in g]))


def halves_kernel(*refs):
    *refs, held, in_sems, out_sems = refs
    count = len(refs) // 2
    half = refs[count].shape[0]
    loads = [
        pltpu.make_async_copy(src.at[pl.ds(i % 2 * half, half)], held.at[i], in_sems.at[i])
        for i, src in enumerate(refs[:count])
    ]
    stores = [
        pltpu.make_async_copy(held.at[i], dst, out_sems.at[i])
        for i, dst in enumerate(refs[count:])
    ]
    for load in loads:
        load.start()
    for load, store in zip(loads, stores):
        load.wait()
        store.start()
    for store in stores:
        store.wait()


def first_and_last_halves(blocks):
    rows, columns = blocks[0].shape
    count, half = len(blocks), rows // 2
    return pl.pallas_call(
        halves_kernel,
        out_shape=[pltpu.HBM((half, columns), b.dtype) for b in blocks],
        in_specs=in_hbm(count),
        out_specs=in_hbm(count),
        scratch_shapes=[
            pltpu.VMEM((count, half, columns), blocks[0].dtype),
            pltpu.SemaphoreType.DMA((count,)),
            pltpu.SemaphoreType.DMA((count,)),
        ],
        compiler_params=pltpu.CompilerParams(vmem_limit_bytes=VMEM_BYTES),
    )(*from_hbm(blocks))


def expert_layer(
    tokens, out_grad, token_flags, routes, route_logits, gate_mat, up_mat, down_mat, group
):
    ring, query_len, doc_len, positions = group
    tok_count, width = tokens.shape
    columns = width + PAD
    ring_z = lax.axis_size("dp") // RING_Y
    number = lax.axis_index("expert").astype(jnp.int32).reshape(1)
    weights = [gate_mat, up_mat, down_mat]
    swapped = [swap_core(w) for w in weights]
    payload = build_payload(tokens, out_grad, token_flags, routes, route_logits, ring_z)
    column, swapped, ring = lax.optimization_barrier((exchange_z(payload), swapped, ring))
    weights = [pltpu.with_memory_space_constraint(w, pltpu.VMEM) for w in weights + swapped]
    half_z = ring_z // 2
    along = column[:half_z].reshape(-1, columns)
    across = column[half_z:].reshape(-1, columns)
    steps = (1, 2, -1)
    along = [along] + [shift_x(along, d) for d in steps]
    across = [across] + [shift_y(across, d) for d in steps]
    ring = ring_start(ring)
    along, across, ring = lax.optimization_barrier((along, across, ring))
    along, across = stack_rows(along, across)
    half = along.shape[0] // 2
    ring = ring_step(ring)
    near_in = [shift_y(along, 1), shift_y(along, -1), shift_x(across, 1), shift_x(across, -1)]
    along_own, across_own = expert_rows([along, across], number, weights)
    near_in, ring = lax.optimization_barrier((near_in, ring))
    halves = first_and_last_halves(near_in)
    halves, along_own, across_own = lax.optimization_barrier((halves, along_own, across_own))
    ring = ring_step(ring)
    far_in = [
        shift_y(halves[0], 1),
        shift_y(halves[1], -1),
        shift_x(halves[2], 1),
        shift_x(halves[3], -1),
    ]
    near = expert_rows(near_in, number, weights)
    far_in, near, ring = lax.optimization_barrier((far_in, near, ring))
    ring = ring_step(ring)
    far = expert_rows(far_in, number, weights, merged=2)
    near = [shift_y(near[0], -1), shift_y(near[1], 1), shift_x(near[2], -1), shift_x(near[3], 1)]
    far, near, ring = lax.optimization_barrier((far, near, ring))
    far = [shift_y(far[0], 2), shift_x(far[1], 2)]
    ring = ring_last(ring)
    far, ring = lax.optimization_barrier((far, ring))
    along_sum, across_sum = add_partials(
        [
            [along_own, near[0], near[1], far[0]],
            [across_own, near[2], near[3], far[1]],
        ],
        pieces=4,
    )
    along_in = [shift_x(b, -d) for b, d in zip(along_sum[1:], steps)]
    across_in = [shift_y(b, -d) for b, d in zip(across_sum[1:], steps)]
    side = contrast(ring_close(ring), query_len, doc_len, positions)
    along_in, across_in, side = lax.optimization_barrier((along_in, across_in, side))
    column = add_last([along_sum[0], *along_in], [across_sum[0], *across_in], tok_count)
    column = exchange_z(column)
    total = jnp.sum(column.astype(jnp.float32), axis=0)
    pair_tok = total[:, width : width + 4].reshape(tok_count, 2, 2).sum(axis=2)
    mixing = jax.nn.softmax(route_logits, axis=-1)
    mean_dot = jnp.sum(mixing * pair_tok, axis=1, keepdims=True)
    return total[:, :width].astype(jnp.bfloat16), mixing * (pair_tok - mean_dot), side


def gather_group(query_states, query_len, doc_states, doc_len, query_pos):
    query_emb = pooled(query_states, query_len)
    doc_emb = pooled(doc_states, doc_len)
    own = query_emb.shape[0]
    positives = jnp.concatenate(
        [
            query_pos[:, None].astype(jnp.bfloat16),
            jnp.zeros((own, PAD - 1), jnp.bfloat16),
        ],
        axis=1,
    )
    rows = jnp.concatenate(
        [
            jnp.concatenate([query_emb, positives], axis=1),
            jnp.concatenate([doc_emb, jnp.zeros_like(positives)], axis=1),
        ],
        axis=0,
    )
    column = [rows] + [shift_y(rows, d) for d in (1, 2, -1)]
    return jnp.concatenate(column, axis=0), query_len, doc_len


def ring_start(mine):
    chip = jnp.concatenate([mine, swap_core(mine)], axis=0)
    return [mine, [], chip]


def ring_step(state):
    mine, arrived, block = state
    if len(arrived) + 1 >= lax.axis_size("dp") // RING_Y // 2:
        return state
    block = shift_outward(block, "z", 1)
    return [mine, arrived + [block], block]


def ring_last(state):
    mine, arrived, block = state
    rows = mine.shape[0]
    return [mine, arrived, shift_outward(block[:rows], "z", 1)]


def ring_close(state):
    mine, arrived, last = state
    rows = mine.shape[0]
    blocks = [mine] + [b[:rows] for b in arrived] + [last]
    if arrived:
        blocks.append(swap_core(jnp.concatenate([b[rows:] for b in arrived], axis=0)))
    return jnp.concatenate(blocks, axis=0)


def contrast_kernel(place_ref, query_len_ref, doc_len_ref, all_ref, query_ref, doc_ref, loss_ref):
    count, columns = all_ref.shape
    width = columns - PAD
    own, positions = query_ref.shape[0], query_ref.shape[1]
    ring_z = count // (2 * own * RING_Y)
    scale_factor = 1.0 / (0.02 * math.sqrt(width))
    embeddings = all_ref[:, :width]
    scores = contract_last(embeddings, embeddings) * scale_factor
    row = lax.broadcasted_iota(jnp.int32, (count, count), 0)
    column = lax.broadcasted_iota(jnp.int32, (count, count), 1)
    query_row = row % (2 * own) < own
    positive = all_ref[:, width:].astype(jnp.float32)[:, 0:1].astype(jnp.int32)
    holder = positive // own
    away_y = (place_ref[1] - holder % RING_Y + RING_Y) % RING_Y
    up = (holder // RING_Y - place_ref[0] + ring_z) % ring_z
    down = (place_ref[0] - holder // RING_Y + ring_z) % ring_z
    away_z = jnp.where(place_ref[2] == 0, down, up)
    away_z = jnp.where(away_z <= ring_z // 2, away_z, ring_z + ring_z // 2 - away_z)
    target = (away_z * RING_Y + away_y) * (2 * own) + own + positive % own
    targets = column == target
    among = jnp.where(column % (2 * own) < own, -jnp.inf, scores)
    highest = jnp.max(among, axis=1, keepdims=True)
    expo = jnp.exp(among - highest)
    totals = jnp.sum(expo, axis=1, keepdims=True)
    lse = highest + jnp.log(totals)
    reached = jnp.sum(jnp.where(targets, scores, 0.0), axis=1, keepdims=True)
    losses = jnp.where(query_row[:, 0:1], lse - reached, 0.0)
    loss_ref[...] = jnp.broadcast_to(jnp.sum(losses, axis=0, keepdims=True), loss_ref.shape)
    coef = (expo / totals - targets.astype(jnp.float32)).astype(jnp.bfloat16)
    coef = jnp.where(query_row, coef.astype(jnp.float32), 0.0)
    mine = (coef + coef.T)[: 2 * own].astype(jnp.bfloat16)
    grads = jnp.dot(mine, embeddings, preferred_element_type=jnp.float32) * scale_factor
    position = lax.broadcasted_iota(jnp.int32, (positions, width), 0)
    for base, lengths, out in ((0, query_len_ref, query_ref), (own, doc_len_ref, doc_ref)):
        for i in range(own):
            length = lengths[i]
            each = grads[base + i : base + i + 1, :] / length.astype(jnp.float32)
            out[i] = jnp.where(position < length, each, 0.0).astype(jnp.bfloat16)


def contrast(everything, query_len, doc_len, positions):
    count, columns = everything.shape
    width, own = columns - PAD, query_len.shape[0]
    dp, expert = lax.axis_index("dp"), lax.axis_index("expert")
    place = jnp.stack([dp // RING_Y, dp % RING_Y, expert % CORES]).astype(jnp.int32)
    grads = jax.ShapeDtypeStruct((own, positions, width), jnp.bfloat16)
    return pl.pallas_call(
        contrast_kernel,
        out_shape=[grads, grads, jax.ShapeDtypeStruct((1, PAD), jnp.float32)],
        in_specs=[*[pl.BlockSpec(memory_space=pltpu.SMEM)] * 3, *in_vmem(1)],
        out_specs=in_vmem(3),
        compiler_params=pltpu.CompilerParams(vmem_limit_bytes=VMEM_BYTES),
        cost_estimate=pl.CostEstimate(
            flops=2 * count * count * width,
            bytes_accessed=2 * count * columns + 4 * own * positions * width,
            transcendentals=count * count,
        ),
    )(place, query_len, doc_len, everything)


def shards(
    tokens,
    out_grad,
    token_flags,
    routes,
    route_logits,
    gate_weight,
    up_weight,
    down_weight,
    query_states,
    query_len,
    doc_states,
    doc_len,
    query_pos,
):
    group = gather_group(
        query_states[0], query_len[0], doc_states[0], doc_len[0], query_pos[0]
    )
    token_grads, logit_grads, side = expert_layer(
        tokens,
        out_grad,
        token_flags,
        routes,
        route_logits,
        gate_weight[0],
        up_weight[0],
        down_weight[0],
        (*group, query_states.shape[2]),
    )
    query_grads, doc_grads, group_loss = side
    losses = lax.all_gather(group_loss, "expert", axis=0, tiled=True)
    queries = query_pos.shape[1] * lax.axis_size("dp") * lax.axis_size("expert")
    loss = jnp.sum(losses[:, 0]) / jnp.float32(queries)
    return (token_grads, logit_grads, query_grads[None], doc_grads[None], loss)


def solution(mesh):
    placed = (
        P(("dp", "expert"), None),
        P(("dp", "expert"), None),
        P(("dp", "expert")),
        P(("dp", "expert"), None),
        P(("dp", "expert"), None),
        P("expert", None, "dp"),
        P("expert", None, "dp"),
        P("expert", "dp", None),
        P("expert", "dp", None, None),
        P("expert", "dp"),
        P("expert", "dp", None, None),
        P("expert", "dp"),
        P("expert", "dp"),
    )
    return jax.shard_map(
        shards,
        mesh=mesh,
        in_specs=placed,
        out_specs=(
            P(("dp", "expert"), None),
            P(("dp", "expert"), None),
            P("expert", "dp", None, None),
            P("expert", "dp", None, None),
            P(),
        ),
        check_vma=False,
    )
```

```python
import math

import jax
import jax.numpy as jnp
from jax import lax
from jax.experimental import pallas as pl
from jax.experimental.pallas import tpu as pltpu
from jax.sharding import PartitionSpec as P

RING_Y = 4
CORES = 2
PAD = 128
VMEM_BYTES = 32 * 1024 * 1024


def contract_last(left, right):
    return lax.dot_general(
        left, right, (((1,), (1,)), ((), ())), preferred_element_type=jnp.float32
    )


def pooled(states, lengths):
    positions = jnp.arange(states.shape[1], dtype=jnp.int32)
    valid = (positions[None, :] < lengths[:, None]).astype(jnp.bfloat16)
    summed = jnp.einsum("qt,qtd->qd", valid, states, preferred_element_type=jnp.float32)
    return (summed / lengths[:, None].astype(jnp.float32)).astype(jnp.bfloat16)


def shift_y(block, step):
    count = lax.axis_size("dp")
    pairs = [
        (i, i // RING_Y * RING_Y + (i % RING_Y + step) % RING_Y) for i in range(count)
    ]
    return lax.ppermute(block, "dp", pairs)


def shift_x(block, step):
    count = lax.axis_size("expert")
    pairs = [(i, (i + step * CORES) % count) for i in range(count)]
    return lax.ppermute(block, "expert", pairs)


def shift_outward(block, axis, step):
    expert_count, count = lax.axis_size("expert"), lax.axis_size("dp")
    pairs = []
    for i in range(count):
        for e in range(expert_count):
            z, y, x, core = i // RING_Y, i % RING_Y, e // CORES, e % CORES
            move = step if core == 0 else -step
            if axis == "z":
                z = (z + move) % (count // RING_Y)
            elif axis == "y":
                y = (y + move) % RING_Y
            else:
                x = (x + move) % (expert_count // CORES)
            target = (z * RING_Y + y) * expert_count + x * CORES + core
            pairs.append((i * expert_count + e, target))
    return lax.ppermute(block, ("dp", "expert"), pairs)


def swap_core(block):
    count = lax.axis_size("expert")
    return lax.ppermute(block, "expert", [(i, i ^ 1) for i in range(count)])


def exchange_z(blocks):
    count = lax.axis_size("dp")
    groups = [list(range(y, count, RING_Y)) for y in range(RING_Y)]
    return lax.all_to_all(blocks, "dp", 0, 0, tiled=True, axis_index_groups=groups)


def in_vmem(count):
    return [pl.BlockSpec(memory_space=pltpu.VMEM)] * count


def in_hbm(count):
    return [pl.BlockSpec(memory_space=pltpu.HBM)] * count


def anywhere(count):
    return [pl.BlockSpec(memory_space=pl.ANY)] * count


def from_hbm(arrays):
    return [pltpu.with_memory_space_constraint(a, pltpu.HBM) for a in arrays]


def high_low(values):
    high = values.astype(jnp.bfloat16).astype(jnp.float32)
    return high, values - high


def at_lanes(rows, columns):
    lane = lax.broadcasted_iota(jnp.int32, (rows, PAD), 1)
    placed = jnp.zeros((rows, PAD), jnp.float32)
    for i, column in enumerate(columns):
        placed = jnp.where(lane == i, column, placed)
    return placed


def payload_kernel(tok_ref, cot_ref, meta_ref, out_ref, held):
    tok_count, width = tok_ref.shape
    meta = meta_ref[...]
    held[:tok_count, :width] = tok_ref[...].astype(jnp.float32)
    held[tok_count:, :width] = jnp.where(
        meta[:, 6:7] == 0, cot_ref[...].astype(jnp.float32), 0.0
    )
    held[:tok_count, width:] = meta
    held[tok_count:, width:] = jnp.zeros((tok_count, PAD), jnp.float32)
    rows = held[...].astype(jnp.bfloat16)
    for i in range(out_ref.shape[0]):
        out_ref[i] = rows


def softmax_of_two(logits):
    first, second = logits[:, 0:1], logits[:, 1:2]
    top = jnp.maximum(first, second)
    first, second = jnp.exp(first - top), jnp.exp(second - top)
    return first / (first + second), second / (first + second)


def build_payload(tokens, out_grad, token_flags, routes, route_logits, copies):
    tok_count, width = tokens.shape
    first, second = softmax_of_two(route_logits)
    meta = at_lanes(
        tok_count,
        [
            routes[:, 0:1].astype(jnp.float32),
            routes[:, 1:2].astype(jnp.float32),
            *high_low(first),
            *high_low(second),
            token_flags[:, None].astype(jnp.float32),
        ],
    )
    return pl.pallas_call(
        payload_kernel,
        out_shape=jax.ShapeDtypeStruct((copies, 2 * tok_count, width + PAD), jnp.bfloat16),
        in_specs=in_vmem(3),
        out_specs=in_vmem(1)[0],
        scratch_shapes=[pltpu.VMEM((2 * tok_count, width + PAD), jnp.float32)],
        compiler_params=pltpu.CompilerParams(vmem_limit_bytes=VMEM_BYTES),
    )(tokens, out_grad, meta)


def expert_kernel(count, merged, number_ref, *refs):
    blocks, refs = refs[:count], refs[count:]
    weights, refs = refs[:6], refs[6:]
    outs, refs = refs[: count // merged], refs[count // merged :]
    sources, inputs, cots, results, in_sems, out_sems = refs
    total_rows, columns = blocks[0].shape
    width = columns - PAD
    rows = total_rows // 2
    loads = [
        pltpu.make_async_copy(
            block, sources.at[pl.ds(i * total_rows, total_rows)], in_sems.at[i]
        )
        for i, block in enumerate(blocks)
    ]
    for load in loads:
        load.start()
    group = min(256, count * total_rows)
    half = group // 2
    row = lax.broadcasted_iota(jnp.int32, (group, group), 0)
    source = lax.broadcasted_iota(jnp.int32, (group, group), 1)
    nth = row % half
    pick = (source == nth // 4 * 8 + nth % 4 + row // half * 4).astype(jnp.bfloat16)
    step = min(width, 512)
    metas = []
    for low in range(0, count * total_rows, group):
        for load in loads[low // total_rows : (low + group) // total_rows]:
            load.wait()
        own = slice(low // 2, low // 2 + half)
        for left in range(0, width, step):
            picked = jnp.dot(
                pick,
                sources[low : low + group, left : left + step],
                preferred_element_type=jnp.float32,
            ).astype(jnp.bfloat16)
            inputs[own, left : left + step] = picked[:half]
            cots[own, left : left + step] = picked[half:]
        metas.append(
            jnp.dot(
                pick, sources[low : low + group, width:], preferred_element_type=jnp.float32
            )[:half]
        )
    meta = jnp.concatenate(metas, axis=0)
    routes = [meta[:, 0:1], meta[:, 1:2]]
    mixing = [meta[:, 2:3] + meta[:, 3:4], meta[:, 4:5] + meta[:, 5:6]]
    number = number_ref[0]
    pairs = [jnp.zeros_like(routes[0]), jnp.zeros_like(routes[0])]
    factors = []
    for e in range(2):
        expert = (number ^ e).astype(jnp.float32)
        taken = [route == expert for route in routes]
        weight = jnp.where(taken[0], mixing[0], jnp.where(taken[1], mixing[1], 0.0))
        gate_mat, up_mat, down_mat = weights[3 * e : 3 * e + 3]
        gate_pre = jnp.dot(inputs[...], gate_mat[...], preferred_element_type=jnp.float32)
        up_pre = jnp.dot(inputs[...], up_mat[...], preferred_element_type=jnp.float32)
        back_hidden = contract_last(cots[...], down_mat[...])
        sigmoid_gate = jax.nn.sigmoid(gate_pre)
        silu = gate_pre * sigmoid_gate
        dots = jnp.sum(back_hidden * silu * up_pre, axis=1, keepdims=True)
        pairs = [p + jnp.where(t, dots, 0.0) for p, t in zip(pairs, taken)]
        back = weight * back_hidden
        gate_grad = back * up_pre * sigmoid_gate * (1.0 + gate_pre * (1.0 - sigmoid_gate))
        factors.append((gate_grad.astype(jnp.bfloat16), gate_mat))
        factors.append(((back * silu).astype(jnp.bfloat16), up_mat))
    each = merged * rows
    stores = []

    def store(low, size):
        for i, out in enumerate(outs):
            copy = pltpu.make_async_copy(
                results.at[pl.ds(i * each, each), pl.ds(low, size)],
                out.at[:, pl.ds(low, size)],
                out_sems.at[low // step, i],
            )
            copy.start()
            stores.append(copy)

    extra = at_lanes(count * rows, [*high_low(pairs[0]), *high_low(pairs[1])])
    results[:, width:] = extra.astype(jnp.bfloat16)
    store(width, PAD)
    for low in range(0, width, step):
        part = sum(contract_last(g, mat[low : low + step, :]) for g, mat in factors)
        results[:, low : low + step] = part.astype(jnp.bfloat16)
        store(low, step)
    for copy in stores:
        copy.wait()


def expert_rows(blocks, number, weights, merged=1):
    count = len(blocks)
    total_rows, columns = blocks[0].shape
    rows, width = total_rows // 2, columns - PAD
    hidden = weights[0].shape[1]
    return pl.pallas_call(
        lambda *refs: expert_kernel(count, merged, *refs),
        out_shape=[pltpu.HBM((merged * rows, columns), jnp.bfloat16)]
        * (count // merged),
        in_specs=[
            pl.BlockSpec(memory_space=pltpu.SMEM),
            *in_hbm(count),
            *in_vmem(6),
        ],
        out_specs=in_hbm(count // merged),
        scratch_shapes=[
            pltpu.VMEM((count * total_rows, columns), jnp.bfloat16),
            pltpu.VMEM((count * rows, width), jnp.bfloat16),
            pltpu.VMEM((count * rows, width), jnp.bfloat16),
            pltpu.VMEM((count * rows, columns), jnp.bfloat16),
            pltpu.SemaphoreType.DMA((count,)),
            pltpu.SemaphoreType.DMA((width // min(width, 512) + 1, count // merged)),
        ],
        compiler_params=pltpu.CompilerParams(vmem_limit_bytes=VMEM_BYTES),
        cost_estimate=pl.CostEstimate(
            flops=20 * count * rows * width * hidden,
            bytes_accessed=12 * width * hidden + 6 * count * rows * columns,
            transcendentals=2 * count * rows * hidden,
        ),
    )(number, *from_hbm(blocks), *weights)


def added(parts):
    width = parts[0].shape[1] - PAD
    total = parts[0][:, :width].astype(jnp.float32)
    extra = parts[0][:, width:].astype(jnp.float32)
    for part in parts[1:]:
        total += part[:, :width].astype(jnp.float32)
        extra += part[:, width:].astype(jnp.float32)
    values = extra + pltpu.roll(extra, PAD - 1, 1)
    high = values.astype(jnp.bfloat16).astype(jnp.float32)
    low = pltpu.roll(values - high, 1, 1)
    lane = lax.broadcasted_iota(jnp.int32, extra.shape, 1)
    kept = jnp.where(lane % 2 == 0, high, low)
    return total, jnp.where(lane < 4, kept, 0.0)


def load_all(refs, held, sems):
    copies = [
        pltpu.make_async_copy(ref, held.at[i], sems.at[i]) for i, ref in enumerate(refs)
    ]
    for copy in copies:
        copy.start()
    return copies


def add_kernel(count, pieces, *refs):
    *refs, held, results, in_sems, out_sems = refs
    groups = len(refs) // (count + pieces)
    outs = refs[count * groups :]
    loads = load_all(refs[: count * groups], held, in_sems)
    width = held.shape[2] - PAD
    size = held.shape[1] // pieces
    stores = []
    for i in range(groups):
        for load in loads[i * count : (i + 1) * count]:
            load.wait()
        total, extra = added([held.at[i * count + j] for j in range(count)])
        results[i, :, :width] = total.astype(jnp.bfloat16)
        results[i, :, width:] = extra.astype(jnp.bfloat16)
        for j, out in enumerate(outs[i * pieces : (i + 1) * pieces]):
            source = results.at[i, pl.ds(j * size, size)]
            store = pltpu.make_async_copy(source, out, out_sems.at[i, j])
            store.start()
            stores.append(store)
    for store in stores:
        store.wait()


def add_last_kernel(count, *refs):
    *refs, out, held, sems = refs
    loads = load_all(refs, held, sems)
    size, width = out.shape[1], out.shape[2] - PAD
    place = 0
    for low in range(0, len(refs), count):
        for load in loads[low : low + count]:
            load.wait()
        total, extra = added([held.at[low + j] for j in range(count)])
        for row in range(0, total.shape[0], size):
            out[place, :, :width] = total[row : row + size].astype(jnp.bfloat16)
            out[place, :, width:] = extra[row : row + size].astype(jnp.bfloat16)
            place += 1


def add_last(first, second, size):
    rows, columns = first[0].shape
    return pl.pallas_call(
        lambda *refs: add_last_kernel(len(first), *refs),
        out_shape=jax.ShapeDtypeStruct((2 * rows // size, size, columns), jnp.bfloat16),
        in_specs=anywhere(2 * len(first)),
        out_specs=in_vmem(1)[0],
        scratch_shapes=[
            pltpu.VMEM((2 * len(first), rows, columns), jnp.bfloat16),
            pltpu.SemaphoreType.DMA((2 * len(first),)),
        ],
        compiler_params=pltpu.CompilerParams(vmem_limit_bytes=VMEM_BYTES),
    )(*first, *second)


def add_partials(groups, pieces=1):
    count, (rows, columns) = len(groups[0]), groups[0][0].shape
    size = len(groups) * rows * columns
    outs = pl.pallas_call(
        lambda *refs: add_kernel(count, pieces, *refs),
        out_shape=[pltpu.HBM((rows // pieces, columns), jnp.bfloat16)] * (len(groups) * pieces),
        in_specs=in_hbm(count * len(groups)),
        out_specs=in_hbm(len(groups) * pieces),
        scratch_shapes=[
            pltpu.VMEM((count * len(groups), rows, columns), jnp.bfloat16),
            pltpu.VMEM((len(groups), rows, columns), jnp.bfloat16),
            pltpu.SemaphoreType.DMA((count * len(groups),)),
            pltpu.SemaphoreType.DMA((len(groups), pieces)),
        ],
        compiler_params=pltpu.CompilerParams(vmem_limit_bytes=VMEM_BYTES),
        cost_estimate=pl.CostEstimate(
            flops=count * size, bytes_accessed=2 * (count + 1) * size, transcendentals=0
        ),
    )(*from_hbm([p for g in groups for p in g]))
    return [outs[i * pieces : (i + 1) * pieces] for i in range(len(groups))]


def stack_kernel(counts, *refs):
    *refs, sems = refs
    blocks, refs = refs[: sum(counts)], refs[sum(counts) :]
    outs, held = refs[: len(counts)], refs[len(counts) :]
    moves, place = [], 0
    for count, out, buffer in zip(counts, outs, held):
        low = 0
        for block in blocks[place : place + count]:
            here = buffer.at[pl.ds(low, block.shape[0])]
            there = out.at[pl.ds(low, block.shape[0])]
            moves.append(
                (
                    pltpu.make_async_copy(block, here, sems.at[0, len(moves)]),
                    pltpu.make_async_copy(here, there, sems.at[1, len(moves)]),
                )
            )
            low += block.shape[0]
        place += count
    for load, _ in moves:
        load.start()
    for load, store in moves:
        load.wait()
        store.start()
    for _, store in moves:
        store.wait()


def stack_rows(*groups):
    counts = [len(g) for g in groups]
    shapes = [(sum(b.shape[0] for b in g), g[0].shape[1]) for g in groups]
    return pl.pallas_call(
        lambda *refs: stack_kernel(counts, *refs),
        out_shape=[pltpu.HBM(s, jnp.bfloat16) for s in shapes],
        in_specs=anywhere(sum(counts)),
        out_specs=in_hbm(len(groups)),
        scratch_shapes=[
            *[pltpu.VMEM(s, jnp.bfloat16) for s in shapes],
            pltpu.SemaphoreType.DMA((2, sum(counts))),
        ],
        compiler_params=pltpu.CompilerParams(vmem_limit_bytes=VMEM_BYTES),
    )(*[b for g in groups for b in g])


def halves_kernel(*refs):
    *refs, held, in_sems, out_sems = refs
    count = len(refs) // 2
    half = refs[count].shape[0]
    loads = [
        pltpu.make_async_copy(src.at[pl.ds(i % 2 * half, half)], held.at[i], in_sems.at[i])
        for i, src in enumerate(refs[:count])
    ]
    stores = [
        pltpu.make_async_copy(held.at[i], dst, out_sems.at[i])
        for i, dst in enumerate(refs[count:])
    ]
    for load in loads:
        load.start()
    for load, store in zip(loads, stores):
        load.wait()
        store.start()
    for store in stores:
        store.wait()


def first_and_last_halves(blocks):
    rows, columns = blocks[0].shape
    count, half = len(blocks), rows // 2
    return pl.pallas_call(
        halves_kernel,
        out_shape=[pltpu.HBM((half, columns), b.dtype) for b in blocks],
        in_specs=in_hbm(count),
        out_specs=in_hbm(count),
        scratch_shapes=[
            pltpu.VMEM((count, half, columns), blocks[0].dtype),
            pltpu.SemaphoreType.DMA((count,)),
            pltpu.SemaphoreType.DMA((count,)),
        ],
        compiler_params=pltpu.CompilerParams(vmem_limit_bytes=VMEM_BYTES),
    )(*from_hbm(blocks))


def expert_layer(
    tokens, out_grad, token_flags, routes, route_logits, gate_mat, up_mat, down_mat, group
):
    ring, query_len, doc_len, positions = group
    tok_count, width = tokens.shape
    columns = width + PAD
    ring_z = lax.axis_size("dp") // RING_Y
    number = lax.axis_index("expert").astype(jnp.int32).reshape(1)
    weights = [gate_mat, up_mat, down_mat]
    swapped = [swap_core(w) for w in weights]
    payload = build_payload(tokens, out_grad, token_flags, routes, route_logits, ring_z)
    column, swapped, ring = lax.optimization_barrier((exchange_z(payload), swapped, ring))
    weights = [pltpu.with_memory_space_constraint(w, pltpu.VMEM) for w in weights + swapped]
    half_z = ring_z // 2
    along = column[:half_z].reshape(-1, columns)
    across = column[half_z:].reshape(-1, columns)
    steps = (1, 2, -1)
    along = [along] + [shift_x(along, d) for d in steps]
    across = [across] + [shift_y(across, d) for d in steps]
    ring = ring_start(ring)
    along, across, ring = lax.optimization_barrier((along, across, ring))
    along, across = stack_rows(along, across)
    half = along.shape[0] // 2
    ring = ring_step(ring)
    near_in = [shift_y(along, 1), shift_y(along, -1), shift_x(across, 1), shift_x(across, -1)]
    along_own, across_own = expert_rows([along, across], number, weights)
    near_in, ring = lax.optimization_barrier((near_in, ring))
    halves = first_and_last_halves(near_in)
    halves, along_own, across_own = lax.optimization_barrier((halves, along_own, across_own))
    ring = ring_step(ring)
    far_in = [
        shift_y(halves[0], 1),
        shift_y(halves[1], -1),
        shift_x(halves[2], 1),
        shift_x(halves[3], -1),
    ]
    near = expert_rows(near_in, number, weights)
    far_in, near, ring = lax.optimization_barrier((far_in, near, ring))
    ring = ring_step(ring)
    far = expert_rows(far_in, number, weights, merged=2)
    near = [shift_y(near[0], -1), shift_y(near[1], 1), shift_x(near[2], -1), shift_x(near[3], 1)]
    far, near, ring = lax.optimization_barrier((far, near, ring))
    far = [shift_y(far[0], 2), shift_x(far[1], 2)]
    ring = ring_last(ring)
    far, ring = lax.optimization_barrier((far, ring))
    along_sum, across_sum = add_partials(
        [
            [along_own, near[0], near[1], far[0]],
            [across_own, near[2], near[3], far[1]],
        ],
        pieces=4,
    )
    along_in = [shift_x(b, -d) for b, d in zip(along_sum[1:], steps)]
    across_in = [shift_y(b, -d) for b, d in zip(across_sum[1:], steps)]
    side = contrast(ring_close(ring), query_len, doc_len, positions)
    along_in, across_in, side = lax.optimization_barrier((along_in, across_in, side))
    column = add_last([along_sum[0], *along_in], [across_sum[0], *across_in], tok_count)
    column = exchange_z(column)
    total = jnp.sum(column.astype(jnp.float32), axis=0)
    pair_tok = total[:, width : width + 4].reshape(tok_count, 2, 2).sum(axis=2)
    mixing = jax.nn.softmax(route_logits, axis=-1)
    mean_dot = jnp.sum(mixing * pair_tok, axis=1, keepdims=True)
    return total[:, :width].astype(jnp.bfloat16), mixing * (pair_tok - mean_dot), side


def gather_group(query_states, query_len, doc_states, doc_len, query_pos):
    query_emb = pooled(query_states, query_len)
    doc_emb = pooled(doc_states, doc_len)
    own = query_emb.shape[0]
    positives = jnp.concatenate(
        [
            query_pos[:, None].astype(jnp.bfloat16),
            jnp.zeros((own, PAD - 1), jnp.bfloat16),
        ],
        axis=1,
    )
    rows = jnp.concatenate(
        [
            jnp.concatenate([query_emb, positives], axis=1),
            jnp.concatenate([doc_emb, jnp.zeros_like(positives)], axis=1),
        ],
        axis=0,
    )
    column = [rows] + [shift_y(rows, d) for d in (1, 2, -1)]
    return jnp.concatenate(column, axis=0), query_len, doc_len


def ring_start(mine):
    chip = jnp.concatenate([mine, swap_core(mine)], axis=0)
    return [mine, [], chip]


def ring_step(state):
    mine, arrived, block = state
    if len(arrived) + 1 >= lax.axis_size("dp") // RING_Y // 2:
        return state
    block = shift_outward(block, "z", 1)
    return [mine, arrived + [block], block]


def ring_last(state):
    mine, arrived, block = state
    return [mine, arrived, shift_outward(block, "z", 1)]


def ring_close(state):
    mine, arrived, last = state
    rows = mine.shape[0]
    blocks = [(mine, 0)] + [(b, 0) for b in arrived] + [(last, 0)]
    return blocks + [(swap_core(b), rows) for b in arrived]


def contrast_kernel(firsts, place_ref, query_len_ref, doc_len_ref, *refs):
    blocks, (query_ref, doc_ref, loss_ref, all_ref, sems) = refs[: len(firsts)], refs[len(firsts) :]
    count, columns = all_ref.shape
    width, rows = columns - PAD, count // len(firsts)
    loads = [
        pltpu.make_async_copy(
            block.at[pl.ds(first, rows)], all_ref.at[pl.ds(i * rows, rows)], sems.at[i]
        )
        for i, (block, first) in enumerate(zip(blocks, firsts))
    ]
    for load in loads:
        load.start()
    for load in loads:
        load.wait()
    own, positions = query_ref.shape[0], query_ref.shape[1]
    ring_z = count // (2 * own * RING_Y)
    scale_factor = 1.0 / (0.02 * math.sqrt(width))
    embeddings = all_ref[:, :width]
    scores = contract_last(embeddings, embeddings) * scale_factor
    row = lax.broadcasted_iota(jnp.int32, (count, count), 0)
    column = lax.broadcasted_iota(jnp.int32, (count, count), 1)
    query_row = row % (2 * own) < own
    positive = all_ref[:, width:].astype(jnp.float32)[:, 0:1].astype(jnp.int32)
    holder = positive // own
    away_y = (place_ref[1] - holder % RING_Y + RING_Y) % RING_Y
    up = (holder // RING_Y - place_ref[0] + ring_z) % ring_z
    down = (place_ref[0] - holder // RING_Y + ring_z) % ring_z
    away_z = jnp.where(place_ref[2] == 0, down, up)
    away_z = jnp.where(away_z <= ring_z // 2, away_z, ring_z + ring_z // 2 - away_z)
    target = (away_z * RING_Y + away_y) * (2 * own) + own + positive % own
    targets = column == target
    among = jnp.where(column % (2 * own) < own, -jnp.inf, scores)
    highest = jnp.max(among, axis=1, keepdims=True)
    expo = jnp.exp(among - highest)
    totals = jnp.sum(expo, axis=1, keepdims=True)
    lse = highest + jnp.log(totals)
    reached = jnp.sum(jnp.where(targets, scores, 0.0), axis=1, keepdims=True)
    losses = jnp.where(query_row[:, 0:1], lse - reached, 0.0)
    loss_ref[...] = jnp.broadcast_to(jnp.sum(losses, axis=0, keepdims=True), loss_ref.shape)
    coef = (expo / totals - targets.astype(jnp.float32)).astype(jnp.bfloat16)
    coef = jnp.where(query_row, coef.astype(jnp.float32), 0.0)
    mine = (coef + coef.T)[: 2 * own].astype(jnp.bfloat16)
    grads = jnp.dot(mine, embeddings, preferred_element_type=jnp.float32) * scale_factor
    position = lax.broadcasted_iota(jnp.int32, (positions, width), 0)
    for base, lengths, out in ((0, query_len_ref, query_ref), (own, doc_len_ref, doc_ref)):
        for i in range(own):
            length = lengths[i]
            each = grads[base + i : base + i + 1, :] / length.astype(jnp.float32)
            out[i] = jnp.where(position < length, each, 0.0).astype(jnp.bfloat16)


def contrast(blocks, query_len, doc_len, positions):
    rows, columns = blocks[0][0].shape
    count = rows * len(blocks)
    width, own = columns - PAD, query_len.shape[0]
    firsts = [first for _, first in blocks]
    dp, expert = lax.axis_index("dp"), lax.axis_index("expert")
    place = jnp.stack([dp // RING_Y, dp % RING_Y, expert % CORES]).astype(jnp.int32)
    grads = jax.ShapeDtypeStruct((own, positions, width), jnp.bfloat16)
    return pl.pallas_call(
        lambda *refs: contrast_kernel(firsts, *refs),
        out_shape=[grads, grads, jax.ShapeDtypeStruct((1, PAD), jnp.float32)],
        in_specs=[*[pl.BlockSpec(memory_space=pltpu.SMEM)] * 3, *anywhere(len(blocks))],
        out_specs=in_vmem(3),
        scratch_shapes=[
            pltpu.VMEM((count, columns), jnp.bfloat16),
            pltpu.SemaphoreType.DMA((len(blocks),)),
        ],
        compiler_params=pltpu.CompilerParams(vmem_limit_bytes=VMEM_BYTES),
        cost_estimate=pl.CostEstimate(
            flops=2 * count * count * width,
            bytes_accessed=2 * count * columns + 4 * own * positions * width,
            transcendentals=count * count,
        ),
    )(place, query_len, doc_len, *[block for block, _ in blocks])


def shards(
    tokens,
    out_grad,
    token_flags,
    routes,
    route_logits,
    gate_weight,
    up_weight,
    down_weight,
    query_states,
    query_len,
    doc_states,
    doc_len,
    query_pos,
):
    group = gather_group(
        query_states[0], query_len[0], doc_states[0], doc_len[0], query_pos[0]
    )
    token_grads, logit_grads, side = expert_layer(
        tokens,
        out_grad,
        token_flags,
        routes,
        route_logits,
        gate_weight[0],
        up_weight[0],
        down_weight[0],
        (*group, query_states.shape[2]),
    )
    query_grads, doc_grads, group_loss = side
    losses = lax.all_gather(group_loss, "expert", axis=0, tiled=True)
    queries = query_pos.shape[1] * lax.axis_size("dp") * lax.axis_size("expert")
    loss = jnp.sum(losses[:, 0]) / jnp.float32(queries)
    return (token_grads, logit_grads, query_grads[None], doc_grads[None], loss)


def solution(mesh):
    placed = (
        P(("dp", "expert"), None),
        P(("dp", "expert"), None),
        P(("dp", "expert")),
        P(("dp", "expert"), None),
        P(("dp", "expert"), None),
        P("expert", None, "dp"),
        P("expert", None, "dp"),
        P("expert", "dp", None),
        P("expert", "dp", None, None),
        P("expert", "dp"),
        P("expert", "dp", None, None),
        P("expert", "dp"),
        P("expert", "dp"),
    )
    return jax.shard_map(
        shards,
        mesh=mesh,
        in_specs=placed,
        out_specs=(
            P(("dp", "expert"), None),
            P(("dp", "expert"), None),
            P("expert", "dp", None, None),
            P("expert", "dp", None, None),
            P(),
        ),
        check_vma=False,
    )
```

```python
import math

import jax
import jax.numpy as jnp
from jax import lax
from jax.experimental import pallas as pl
from jax.experimental.pallas import tpu as pltpu
from jax.sharding import PartitionSpec as P

RING_Y = 4
CORES = 2
PAD = 128
VMEM_BYTES = 32 * 1024 * 1024


def contract_last(left, right):
    return lax.dot_general(
        left, right, (((1,), (1,)), ((), ())), preferred_element_type=jnp.float32
    )


def pooled(states, lengths):
    positions = jnp.arange(states.shape[1], dtype=jnp.int32)
    valid = (positions[None, :] < lengths[:, None]).astype(jnp.bfloat16)
    summed = jnp.einsum("qt,qtd->qd", valid, states, preferred_element_type=jnp.float32)
    return (summed / lengths[:, None].astype(jnp.float32)).astype(jnp.bfloat16)


def shift_y(block, step):
    count = lax.axis_size("dp")
    pairs = [
        (i, i // RING_Y * RING_Y + (i % RING_Y + step) % RING_Y) for i in range(count)
    ]
    return lax.ppermute(block, "dp", pairs)


def shift_x(block, step):
    count = lax.axis_size("expert")
    pairs = [(i, (i + step * CORES) % count) for i in range(count)]
    return lax.ppermute(block, "expert", pairs)


def shift_outward(block, axis, step):
    expert_count, count = lax.axis_size("expert"), lax.axis_size("dp")
    pairs = []
    for i in range(count):
        for e in range(expert_count):
            z, y, x, core = i // RING_Y, i % RING_Y, e // CORES, e % CORES
            move = step if core == 0 else -step
            if axis == "z":
                z = (z + move) % (count // RING_Y)
            elif axis == "y":
                y = (y + move) % RING_Y
            else:
                x = (x + move) % (expert_count // CORES)
            target = (z * RING_Y + y) * expert_count + x * CORES + core
            pairs.append((i * expert_count + e, target))
    return lax.ppermute(block, ("dp", "expert"), pairs)


def swap_core(block):
    count = lax.axis_size("expert")
    return lax.ppermute(block, "expert", [(i, i ^ 1) for i in range(count)])


def exchange_z(blocks):
    count = lax.axis_size("dp")
    groups = [list(range(y, count, RING_Y)) for y in range(RING_Y)]
    return lax.all_to_all(blocks, "dp", 0, 0, tiled=True, axis_index_groups=groups)


def in_vmem(count):
    return [pl.BlockSpec(memory_space=pltpu.VMEM)] * count


def in_hbm(count):
    return [pl.BlockSpec(memory_space=pltpu.HBM)] * count


def anywhere(count):
    return [pl.BlockSpec(memory_space=pl.ANY)] * count


def from_hbm(arrays):
    return [pltpu.with_memory_space_constraint(a, pltpu.HBM) for a in arrays]


def high_low(values):
    high = values.astype(jnp.bfloat16).astype(jnp.float32)
    return high, values - high


def at_lanes(rows, columns):
    lane = lax.broadcasted_iota(jnp.int32, (rows, PAD), 1)
    placed = jnp.zeros((rows, PAD), jnp.float32)
    for i, column in enumerate(columns):
        placed = jnp.where(lane == i, column, placed)
    return placed


def payload_kernel(tok_ref, cot_ref, meta_ref, out_ref, held):
    tok_count, width = tok_ref.shape
    meta = meta_ref[...]
    held[:tok_count, :width] = tok_ref[...].astype(jnp.float32)
    held[tok_count:, :width] = jnp.where(
        meta[:, 6:7] == 0, cot_ref[...].astype(jnp.float32), 0.0
    )
    held[:tok_count, width:] = meta
    held[tok_count:, width:] = jnp.zeros((tok_count, PAD), jnp.float32)
    rows = held[...].astype(jnp.bfloat16)
    for i in range(out_ref.shape[0]):
        out_ref[i] = rows


def softmax_of_two(logits):
    first, second = logits[:, 0:1], logits[:, 1:2]
    top = jnp.maximum(first, second)
    first, second = jnp.exp(first - top), jnp.exp(second - top)
    return first / (first + second), second / (first + second)


def build_payload(tokens, out_grad, token_flags, routes, route_logits, copies):
    tok_count, width = tokens.shape
    first, second = softmax_of_two(route_logits)
    meta = at_lanes(
        tok_count,
        [
            routes[:, 0:1].astype(jnp.float32),
            routes[:, 1:2].astype(jnp.float32),
            *high_low(first),
            *high_low(second),
            token_flags[:, None].astype(jnp.float32),
        ],
    )
    return pl.pallas_call(
        payload_kernel,
        out_shape=jax.ShapeDtypeStruct((copies, 2 * tok_count, width + PAD), jnp.bfloat16),
        in_specs=in_vmem(3),
        out_specs=in_vmem(1)[0],
        scratch_shapes=[pltpu.VMEM((2 * tok_count, width + PAD), jnp.float32)],
        compiler_params=pltpu.CompilerParams(vmem_limit_bytes=VMEM_BYTES),
    )(tokens, out_grad, meta)


def expert_kernel(count, merged, number_ref, *refs):
    blocks, refs = refs[:count], refs[count:]
    weights, refs = refs[:6], refs[6:]
    outs, refs = refs[: count // merged], refs[count // merged :]
    sources, inputs, cots, results, in_sems, out_sems = refs
    total_rows, columns = blocks[0].shape
    width = columns - PAD
    rows = total_rows // 2
    loads = [
        pltpu.make_async_copy(
            block, sources.at[pl.ds(i * total_rows, total_rows)], in_sems.at[i]
        )
        for i, block in enumerate(blocks)
    ]
    for load in loads:
        load.start()
    group = min(256, count * total_rows)
    half = group // 2
    row = lax.broadcasted_iota(jnp.int32, (group, group), 0)
    source = lax.broadcasted_iota(jnp.int32, (group, group), 1)
    nth = row % half
    pick = (source == nth // 4 * 8 + nth % 4 + row // half * 4).astype(jnp.bfloat16)
    step = min(width, 1024)
    metas = []
    for low in range(0, count * total_rows, group):
        for load in loads[low // total_rows : (low + group) // total_rows]:
            load.wait()
        own = slice(low // 2, low // 2 + half)
        for left in range(0, width, step):
            picked = jnp.dot(
                pick,
                sources[low : low + group, left : left + step],
                preferred_element_type=jnp.float32,
            ).astype(jnp.bfloat16)
            inputs[own, left : left + step] = picked[:half]
            cots[own, left : left + step] = picked[half:]
        metas.append(
            jnp.dot(
                pick, sources[low : low + group, width:], preferred_element_type=jnp.float32
            )[:half]
        )
    meta = jnp.concatenate(metas, axis=0)
    routes = [meta[:, 0:1], meta[:, 1:2]]
    mixing = [meta[:, 2:3] + meta[:, 3:4], meta[:, 4:5] + meta[:, 5:6]]
    number = number_ref[0]
    pairs = [jnp.zeros_like(routes[0]), jnp.zeros_like(routes[0])]
    factors = []
    for e in range(2):
        expert = (number ^ e).astype(jnp.float32)
        taken = [route == expert for route in routes]
        weight = jnp.where(taken[0], mixing[0], jnp.where(taken[1], mixing[1], 0.0))
        gate_mat, up_mat, down_mat = weights[3 * e : 3 * e + 3]
        gate_pre = jnp.dot(inputs[...], gate_mat[...], preferred_element_type=jnp.float32)
        up_pre = jnp.dot(inputs[...], up_mat[...], preferred_element_type=jnp.float32)
        back_hidden = contract_last(cots[...], down_mat[...])
        sigmoid_gate = jax.nn.sigmoid(gate_pre)
        silu = gate_pre * sigmoid_gate
        dots = jnp.sum(back_hidden * silu * up_pre, axis=1, keepdims=True)
        pairs = [p + jnp.where(t, dots, 0.0) for p, t in zip(pairs, taken)]
        back = weight * back_hidden
        gate_grad = back * up_pre * sigmoid_gate * (1.0 + gate_pre * (1.0 - sigmoid_gate))
        factors.append((gate_grad.astype(jnp.bfloat16), gate_mat))
        factors.append(((back * silu).astype(jnp.bfloat16), up_mat))
    each = merged * rows
    stores = []

    def store(low, size):
        for i, out in enumerate(outs):
            copy = pltpu.make_async_copy(
                results.at[pl.ds(i * each, each), pl.ds(low, size)],
                out.at[:, pl.ds(low, size)],
                out_sems.at[low // step, i],
            )
            copy.start()
            stores.append(copy)

    extra = at_lanes(count * rows, [*high_low(pairs[0]), *high_low(pairs[1])])
    results[:, width:] = extra.astype(jnp.bfloat16)
    store(width, PAD)
    for low in range(0, width, step):
        part = sum(contract_last(g, mat[low : low + step, :]) for g, mat in factors)
        results[:, low : low + step] = part.astype(jnp.bfloat16)
        store(low, step)
    for copy in stores:
        copy.wait()


def expert_rows(blocks, number, weights, merged=1):
    count = len(blocks)
    total_rows, columns = blocks[0].shape
    rows, width = total_rows // 2, columns - PAD
    hidden = weights[0].shape[1]
    return pl.pallas_call(
        lambda *refs: expert_kernel(count, merged, *refs),
        out_shape=[pltpu.HBM((merged * rows, columns), jnp.bfloat16)]
        * (count // merged),
        in_specs=[
            pl.BlockSpec(memory_space=pltpu.SMEM),
            *in_hbm(count),
            *in_vmem(6),
        ],
        out_specs=in_hbm(count // merged),
        scratch_shapes=[
            pltpu.VMEM((count * total_rows, columns), jnp.bfloat16),
            pltpu.VMEM((count * rows, width), jnp.bfloat16),
            pltpu.VMEM((count * rows, width), jnp.bfloat16),
            pltpu.VMEM((count * rows, columns), jnp.bfloat16),
            pltpu.SemaphoreType.DMA((count,)),
            pltpu.SemaphoreType.DMA((width // min(width, 1024) + 1, count // merged)),
        ],
        compiler_params=pltpu.CompilerParams(vmem_limit_bytes=VMEM_BYTES),
        cost_estimate=pl.CostEstimate(
            flops=20 * count * rows * width * hidden,
            bytes_accessed=12 * width * hidden + 6 * count * rows * columns,
            transcendentals=2 * count * rows * hidden,
        ),
    )(number, *from_hbm(blocks), *weights)


def added(parts):
    width = parts[0].shape[1] - PAD
    total = parts[0][:, :width].astype(jnp.float32)
    extra = parts[0][:, width:].astype(jnp.float32)
    for part in parts[1:]:
        total += part[:, :width].astype(jnp.float32)
        extra += part[:, width:].astype(jnp.float32)
    values = extra + pltpu.roll(extra, PAD - 1, 1)
    high = values.astype(jnp.bfloat16).astype(jnp.float32)
    low = pltpu.roll(values - high, 1, 1)
    lane = lax.broadcasted_iota(jnp.int32, extra.shape, 1)
    kept = jnp.where(lane % 2 == 0, high, low)
    return total, jnp.where(lane < 4, kept, 0.0)


def load_all(refs, held, sems):
    copies = [
        pltpu.make_async_copy(ref, held.at[i], sems.at[i]) for i, ref in enumerate(refs)
    ]
    for copy in copies:
        copy.start()
    return copies


def add_kernel(count, pieces, *refs):
    *refs, held, results, in_sems, out_sems = refs
    groups = len(refs) // (count + pieces)
    outs = refs[count * groups :]
    loads = [
        pltpu.make_async_copy(ref, held.at[i], in_sems.at[i])
        for i, ref in enumerate(refs[: count * groups])
    ]
    for load in loads[:count]:
        load.start()
    width = held.shape[2] - PAD
    size = held.shape[1] // pieces
    stores = []
    for i in range(groups):
        for load in loads[i * count : (i + 1) * count]:
            load.wait()
        for load in loads[(i + 1) * count : (i + 2) * count]:
            load.start()
        total, extra = added([held.at[i * count + j] for j in range(count)])
        results[i, :, :width] = total.astype(jnp.bfloat16)
        results[i, :, width:] = extra.astype(jnp.bfloat16)
        for j, out in enumerate(outs[i * pieces : (i + 1) * pieces]):
            source = results.at[i, pl.ds(j * size, size)]
            store = pltpu.make_async_copy(source, out, out_sems.at[i, j])
            store.start()
            stores.append(store)
    for store in stores:
        store.wait()


def add_last_kernel(count, *refs):
    *refs, out, held, sems = refs
    loads = load_all(refs, held, sems)
    size, width = out.shape[1], out.shape[2] - PAD
    place = 0
    for low in range(0, len(refs), count):
        for load in loads[low : low + count]:
            load.wait()
        total, extra = added([held.at[low + j] for j in range(count)])
        for row in range(0, total.shape[0], size):
            out[place, :, :width] = total[row : row + size].astype(jnp.bfloat16)
            out[place, :, width:] = extra[row : row + size].astype(jnp.bfloat16)
            place += 1


def add_last(first, second, size):
    rows, columns = first[0].shape
    return pl.pallas_call(
        lambda *refs: add_last_kernel(len(first), *refs),
        out_shape=jax.ShapeDtypeStruct((2 * rows // size, size, columns), jnp.bfloat16),
        in_specs=anywhere(2 * len(first)),
        out_specs=in_vmem(1)[0],
        scratch_shapes=[
            pltpu.VMEM((2 * len(first), rows, columns), jnp.bfloat16),
            pltpu.SemaphoreType.DMA((2 * len(first),)),
        ],
        compiler_params=pltpu.CompilerParams(vmem_limit_bytes=VMEM_BYTES),
    )(*first, *second)


def add_partials(groups, pieces=1):
    count, (rows, columns) = len(groups[0]), groups[0][0].shape
    size = len(groups) * rows * columns
    outs = pl.pallas_call(
        lambda *refs: add_kernel(count, pieces, *refs),
        out_shape=[pltpu.HBM((rows // pieces, columns), jnp.bfloat16)] * (len(groups) * pieces),
        in_specs=in_hbm(count * len(groups)),
        out_specs=in_hbm(len(groups) * pieces),
        scratch_shapes=[
            pltpu.VMEM((count * len(groups), rows, columns), jnp.bfloat16),
            pltpu.VMEM((len(groups), rows, columns), jnp.bfloat16),
            pltpu.SemaphoreType.DMA((count * len(groups),)),
            pltpu.SemaphoreType.DMA((len(groups), pieces)),
        ],
        compiler_params=pltpu.CompilerParams(vmem_limit_bytes=VMEM_BYTES),
        cost_estimate=pl.CostEstimate(
            flops=count * size, bytes_accessed=2 * (count + 1) * size, transcendentals=0
        ),
    )(*from_hbm([p for g in groups for p in g]))
    return [outs[i * pieces : (i + 1) * pieces] for i in range(len(groups))]


def stack_kernel(counts, *refs):
    *refs, sems = refs
    blocks, refs = refs[: sum(counts)], refs[sum(counts) :]
    outs, held = refs[: len(counts)], refs[len(counts) :]
    moves, place = [], 0
    for count, out, buffer in zip(counts, outs, held):
        low = 0
        for block in blocks[place : place + count]:
            here = buffer.at[pl.ds(low, block.shape[0])]
            there = out.at[pl.ds(low, block.shape[0])]
            moves.append(
                (
                    pltpu.make_async_copy(block, here, sems.at[0, len(moves)]),
                    pltpu.make_async_copy(here, there, sems.at[1, len(moves)]),
                )
            )
            low += block.shape[0]
        place += count
    for load, _ in moves:
        load.start()
    for load, store in moves:
        load.wait()
        store.start()
    for _, store in moves:
        store.wait()


def stack_rows(*groups):
    counts = [len(g) for g in groups]
    shapes = [(sum(b.shape[0] for b in g), g[0].shape[1]) for g in groups]
    return pl.pallas_call(
        lambda *refs: stack_kernel(counts, *refs),
        out_shape=[pltpu.HBM(s, jnp.bfloat16) for s in shapes],
        in_specs=anywhere(sum(counts)),
        out_specs=in_hbm(len(groups)),
        scratch_shapes=[
            *[pltpu.VMEM(s, jnp.bfloat16) for s in shapes],
            pltpu.SemaphoreType.DMA((2, sum(counts))),
        ],
        compiler_params=pltpu.CompilerParams(vmem_limit_bytes=VMEM_BYTES),
    )(*[b for g in groups for b in g])


def halves_kernel(*refs):
    *refs, held, in_sems, out_sems = refs
    count = len(refs) // 2
    half = refs[count].shape[0]
    loads = [
        pltpu.make_async_copy(src.at[pl.ds(i % 2 * half, half)], held.at[i], in_sems.at[i])
        for i, src in enumerate(refs[:count])
    ]
    stores = [
        pltpu.make_async_copy(held.at[i], dst, out_sems.at[i])
        for i, dst in enumerate(refs[count:])
    ]
    for load in loads:
        load.start()
    for load, store in zip(loads, stores):
        load.wait()
        store.start()
    for store in stores:
        store.wait()


def first_and_last_halves(blocks):
    rows, columns = blocks[0].shape
    count, half = len(blocks), rows // 2
    return pl.pallas_call(
        halves_kernel,
        out_shape=[pltpu.HBM((half, columns), b.dtype) for b in blocks],
        in_specs=in_hbm(count),
        out_specs=in_hbm(count),
        scratch_shapes=[
            pltpu.VMEM((count, half, columns), blocks[0].dtype),
            pltpu.SemaphoreType.DMA((count,)),
            pltpu.SemaphoreType.DMA((count,)),
        ],
        compiler_params=pltpu.CompilerParams(vmem_limit_bytes=VMEM_BYTES),
    )(*from_hbm(blocks))


def expert_layer(
    tokens, out_grad, token_flags, routes, route_logits, gate_mat, up_mat, down_mat, group
):
    ring, query_len, doc_len, positions = group
    tok_count, width = tokens.shape
    columns = width + PAD
    ring_z = lax.axis_size("dp") // RING_Y
    number = lax.axis_index("expert").astype(jnp.int32).reshape(1)
    weights = [gate_mat, up_mat, down_mat]
    swapped = [swap_core(w) for w in weights]
    payload = build_payload(tokens, out_grad, token_flags, routes, route_logits, ring_z)
    column, swapped, ring = lax.optimization_barrier((exchange_z(payload), swapped, ring))
    weights = [pltpu.with_memory_space_constraint(w, pltpu.VMEM) for w in weights + swapped]
    half_z = ring_z // 2
    along = column[:half_z].reshape(-1, columns)
    across = column[half_z:].reshape(-1, columns)
    steps = (1, 2, -1)
    along = [along] + [shift_x(along, d) for d in steps]
    across = [across] + [shift_y(across, d) for d in steps]
    ring = ring_start(ring)
    along, across, ring = lax.optimization_barrier((along, across, ring))
    along, across = stack_rows(along, across)
    half = along.shape[0] // 2
    ring = ring_step(ring)
    near_in = [shift_y(along, 1), shift_y(along, -1), shift_x(across, 1), shift_x(across, -1)]
    along_own, across_own = expert_rows([along, across], number, weights)
    near_in, ring = lax.optimization_barrier((near_in, ring))
    halves = first_and_last_halves(near_in)
    halves, along_own, across_own = lax.optimization_barrier((halves, along_own, across_own))
    ring = ring_step(ring)
    far_in = [
        shift_y(halves[0], 1),
        shift_y(halves[1], -1),
        shift_x(halves[2], 1),
        shift_x(halves[3], -1),
    ]
    near = expert_rows(near_in, number, weights)
    far_in, near, ring = lax.optimization_barrier((far_in, near, ring))
    ring = ring_step(ring)
    far = expert_rows(far_in, number, weights, merged=2)
    near = [shift_y(near[0], -1), shift_y(near[1], 1), shift_x(near[2], -1), shift_x(near[3], 1)]
    far, near, ring = lax.optimization_barrier((far, near, ring))
    far = [shift_y(far[0], 2), shift_x(far[1], 2)]
    ring = ring_last(ring)
    far, ring = lax.optimization_barrier((far, ring))
    along_sum, across_sum = add_partials(
        [
            [along_own, near[0], near[1], far[0]],
            [across_own, near[2], near[3], far[1]],
        ],
        pieces=4,
    )
    along_in = [shift_x(b, -d) for b, d in zip(along_sum[1:], steps)]
    across_in = [shift_y(b, -d) for b, d in zip(across_sum[1:], steps)]
    side = contrast(ring_close(ring), query_len, doc_len, positions)
    along_in, across_in, side = lax.optimization_barrier((along_in, across_in, side))
    column = add_last([along_sum[0], *along_in], [across_sum[0], *across_in], tok_count)
    column = exchange_z(column)
    total = jnp.sum(column.astype(jnp.float32), axis=0)
    pair_tok = total[:, width : width + 4].reshape(tok_count, 2, 2).sum(axis=2)
    mixing = jax.nn.softmax(route_logits, axis=-1)
    mean_dot = jnp.sum(mixing * pair_tok, axis=1, keepdims=True)
    return total[:, :width].astype(jnp.bfloat16), mixing * (pair_tok - mean_dot), side


def gather_group(query_states, query_len, doc_states, doc_len, query_pos):
    query_emb = pooled(query_states, query_len)
    doc_emb = pooled(doc_states, doc_len)
    own = query_emb.shape[0]
    positives = jnp.concatenate(
        [
            query_pos[:, None].astype(jnp.bfloat16),
            jnp.zeros((own, PAD - 1), jnp.bfloat16),
        ],
        axis=1,
    )
    rows = jnp.concatenate(
        [
            jnp.concatenate([query_emb, positives], axis=1),
            jnp.concatenate([doc_emb, jnp.zeros_like(positives)], axis=1),
        ],
        axis=0,
    )
    column = [rows] + [shift_y(rows, d) for d in (1, 2, -1)]
    return jnp.concatenate(column, axis=0), query_len, doc_len


def ring_start(mine):
    chip = jnp.concatenate([mine, swap_core(mine)], axis=0)
    return [mine, [], chip]


def ring_step(state):
    mine, arrived, block = state
    if len(arrived) + 1 >= lax.axis_size("dp") // RING_Y // 2:
        return state
    block = shift_outward(block, "z", 1)
    return [mine, arrived + [block], block]


def ring_last(state):
    mine, arrived, block = state
    return [mine, arrived, shift_outward(block, "z", 1)]


def ring_close(state):
    mine, arrived, last = state
    rows = mine.shape[0]
    blocks = [(mine, 0)] + [(b, 0) for b in arrived] + [(last, 0)]
    return blocks + [(swap_core(b), rows) for b in arrived]


def contrast_kernel(firsts, place_ref, query_len_ref, doc_len_ref, *refs):
    blocks, (query_ref, doc_ref, loss_ref, all_ref, sems) = refs[: len(firsts)], refs[len(firsts) :]
    count, columns = all_ref.shape
    width, rows = columns - PAD, count // len(firsts)
    loads = [
        pltpu.make_async_copy(
            block.at[pl.ds(first, rows)], all_ref.at[pl.ds(i * rows, rows)], sems.at[i]
        )
        for i, (block, first) in enumerate(zip(blocks, firsts))
    ]
    for load in loads:
        load.start()
    for load in loads:
        load.wait()
    own, positions = query_ref.shape[0], query_ref.shape[1]
    ring_z = count // (2 * own * RING_Y)
    scale_factor = 1.0 / (0.02 * math.sqrt(width))
    embeddings = all_ref[:, :width]
    scores = contract_last(embeddings, embeddings) * scale_factor
    row = lax.broadcasted_iota(jnp.int32, (count, count), 0)
    column = lax.broadcasted_iota(jnp.int32, (count, count), 1)
    query_row = row % (2 * own) < own
    positive = all_ref[:, width:].astype(jnp.float32)[:, 0:1].astype(jnp.int32)
    holder = positive // own
    away_y = (place_ref[1] - holder % RING_Y + RING_Y) % RING_Y
    up = (holder // RING_Y - place_ref[0] + ring_z) % ring_z
    down = (place_ref[0] - holder // RING_Y + ring_z) % ring_z
    away_z = jnp.where(place_ref[2] == 0, down, up)
    away_z = jnp.where(away_z <= ring_z // 2, away_z, ring_z + ring_z // 2 - away_z)
    target = (away_z * RING_Y + away_y) * (2 * own) + own + positive % own
    targets = column == target
    among = jnp.where(column % (2 * own) < own, -jnp.inf, scores)
    highest = jnp.max(among, axis=1, keepdims=True)
    expo = jnp.exp(among - highest)
    totals = jnp.sum(expo, axis=1, keepdims=True)
    lse = highest + jnp.log(totals)
    reached = jnp.sum(jnp.where(targets, scores, 0.0), axis=1, keepdims=True)
    losses = jnp.where(query_row[:, 0:1], lse - reached, 0.0)
    loss_ref[...] = jnp.broadcast_to(jnp.sum(losses, axis=0, keepdims=True), loss_ref.shape)
    coef = (expo / totals - targets.astype(jnp.float32)).astype(jnp.bfloat16)
    coef = jnp.where(query_row, coef.astype(jnp.float32), 0.0)
    mine = (coef + coef.T)[: 2 * own].astype(jnp.bfloat16)
    grads = jnp.dot(mine, embeddings, preferred_element_type=jnp.float32) * scale_factor
    position = lax.broadcasted_iota(jnp.int32, (positions, width), 0)
    for base, lengths, out in ((0, query_len_ref, query_ref), (own, doc_len_ref, doc_ref)):
        for i in range(own):
            length = lengths[i]
            each = grads[base + i : base + i + 1, :] / length.astype(jnp.float32)
            out[i] = jnp.where(position < length, each, 0.0).astype(jnp.bfloat16)


def contrast(blocks, query_len, doc_len, positions):
    rows, columns = blocks[0][0].shape
    count = rows * len(blocks)
    width, own = columns - PAD, query_len.shape[0]
    firsts = [first for _, first in blocks]
    dp, expert = lax.axis_index("dp"), lax.axis_index("expert")
    place = jnp.stack([dp // RING_Y, dp % RING_Y, expert % CORES]).astype(jnp.int32)
    grads = jax.ShapeDtypeStruct((own, positions, width), jnp.bfloat16)
    return pl.pallas_call(
        lambda *refs: contrast_kernel(firsts, *refs),
        out_shape=[grads, grads, jax.ShapeDtypeStruct((1, PAD), jnp.float32)],
        in_specs=[*[pl.BlockSpec(memory_space=pltpu.SMEM)] * 3, *anywhere(len(blocks))],
        out_specs=in_vmem(3),
        scratch_shapes=[
            pltpu.VMEM((count, columns), jnp.bfloat16),
            pltpu.SemaphoreType.DMA((len(blocks),)),
        ],
        compiler_params=pltpu.CompilerParams(vmem_limit_bytes=VMEM_BYTES),
        cost_estimate=pl.CostEstimate(
            flops=2 * count * count * width,
            bytes_accessed=2 * count * columns + 4 * own * positions * width,
            transcendentals=count * count,
        ),
    )(place, query_len, doc_len, *[block for block, _ in blocks])


def shards(
    tokens,
    out_grad,
    token_flags,
    routes,
    route_logits,
    gate_weight,
    up_weight,
    down_weight,
    query_states,
    query_len,
    doc_states,
    doc_len,
    query_pos,
):
    group = gather_group(
        query_states[0], query_len[0], doc_states[0], doc_len[0], query_pos[0]
    )
    token_grads, logit_grads, side = expert_layer(
        tokens,
        out_grad,
        token_flags,
        routes,
        route_logits,
        gate_weight[0],
        up_weight[0],
        down_weight[0],
        (*group, query_states.shape[2]),
    )
    query_grads, doc_grads, group_loss = side
    losses = lax.all_gather(group_loss, "expert", axis=0, tiled=True)
    queries = query_pos.shape[1] * lax.axis_size("dp") * lax.axis_size("expert")
    loss = jnp.sum(losses[:, 0]) / jnp.float32(queries)
    return (token_grads, logit_grads, query_grads[None], doc_grads[None], loss)


def solution(mesh):
    placed = (
        P(("dp", "expert"), None),
        P(("dp", "expert"), None),
        P(("dp", "expert")),
        P(("dp", "expert"), None),
        P(("dp", "expert"), None),
        P("expert", None, "dp"),
        P("expert", None, "dp"),
        P("expert", "dp", None),
        P("expert", "dp", None, None),
        P("expert", "dp"),
        P("expert", "dp", None, None),
        P("expert", "dp"),
        P("expert", "dp"),
    )
    return jax.shard_map(
        shards,
        mesh=mesh,
        in_specs=placed,
        out_specs=(
            P(("dp", "expert"), None),
            P(("dp", "expert"), None),
            P("expert", "dp", None, None),
            P("expert", "dp", None, None),
            P(),
        ),
        check_vma=False,
    )
```
